512 devices in a mesh: dp: 8 (over z_lo), ep: 64 (over x, y, z_hi, core).
Axes of the slice: x: 4, y: 4, z: 16 (z_hi: 2, z_lo: 8; z = z_hi * 8 + z_lo), core: 2. Of those that a mesh axis runs over, the one named last changes fastest.
Arguments:
- tokens: bfloat16 [2, 3072, 4096], P(None, ('dp', 'ep')), may hold values from -6 to 6
- experts: int32 [2, 3072, 8], P(None, ('dp', 'ep')), may hold values from 0 to 55, all different within a row; in each aligned block of 6 rows (0 to 5, 6 to 11, ..., all dimensions but the last counted through in order) at most 2 rows name the same one
- replicas: int32 [2, 3072, 8], P(None, ('dp', 'ep')), may hold values from 0 to 1
- route_weights: float32 [2, 3072, 8], P(None, ('dp', 'ep')), may hold values from 0.1 to 0.5
- slot_tables: int32 [2, 56, 2], replicated, may hold values from 0 to 63, as said below
- partners: int32 [64], replicated, may hold values from 0 to 63, as said below
- slot_rows: int32 [2, 8, 64], replicated, may hold values from 24 to 48, as said below
- gate_w: bfloat16 [64, 4096, 1024], P('ep', None, 'dp'), may hold values from -0.09375 to 0.09375
- up_w: bfloat16 [64, 4096, 1024], P('ep', None, 'dp'), may hold values from -0.09375 to 0.09375
- down_w: bfloat16 [64, 1024, 4096], P('ep', None, 'dp'), may hold values from -0.1875 to 0.1875
Outputs:
- mixed: bfloat16 [2, 3072, 4096], P(None, ('dp', 'ep'))
The draws below stay inside these ranges and needn't reach their ends.
Inputs may be any that keep to these rules, and one draw needn't show every extreme that they name: `experts`: in each step, the 6 tokens of one device name one expert at most 2 times. slot_tables[0] gives each expert a slot in column 0; 8 experts have a second slot in column 1, the others repeat column 0; every slot appears exactly once as a column 0 entry or a second slot. slot_tables[1][e, c] = partners[slot_tables[0][e, c]]. partners[partners[s]] = s, and partners[s] is s or s plus or minus 64 // 2; partners[0] = 32. `slot_rows`: each step has some entry equal to 48.
All inputs are finite; a program needn't handle non-finite values.
Results may differ from the reference program's by a relative error of at most 0.0058.
Values may be sent and summed in bfloat16 or wider, within the bound.
No kernel may reach another device: no remote copies, remote signals or barrier semaphores. Data moves between devices by JAX's collectives and lax.ppermute only.
A program may use at most 64 MiB of HBM per device.

```python
import math
import jax
import jax.numpy as jnp
import numpy as np
from jax import lax

D = 4096
HID = 1024
TOP = 8
TOK_DEV = 6
SLOTS = 64
RED = 8
EXPERTS = 56
TOKENS = 3072
MOST = 2
CAP = 48
N_DP = 8


def plan_tables(key):
    first_key, second_key, third_key = jax.random.split(key, 3)
    count = SLOTS - RED
    order = jax.random.permutation(first_key, SLOTS).astype(jnp.int32)
    popular = jax.random.permutation(second_key, count)[:RED].astype(jnp.int32)
    flags = jax.random.randint(third_key, (SLOTS // 2,), 0, 2).astype(jnp.int32)
    flags = jnp.where(jnp.arange(SLOTS // 2, dtype=jnp.int32) == 0, 1, flags).astype(jnp.int32)
    labels = jnp.arange(count, dtype=jnp.int32)
    match = labels[:, None] == popular[None, :]
    extra = jnp.sum(jnp.where(match, order[count:][None, :], 0), axis=1).astype(jnp.int32)
    primary = order[:count]
    second = jnp.where(jnp.any(match, axis=1), extra, primary)
    table_now = jnp.stack([primary, second], axis=1)
    half = SLOTS // 2
    index = jnp.arange(SLOTS, dtype=jnp.int32)
    flag_all = jnp.concatenate([flags, flags])
    across = jnp.where(index < half, index + half, index - half)
    partner = jnp.where(flag_all == 1, across, index).astype(jnp.int32)
    table_next = partner[table_now]
    return (jnp.stack([table_now, table_next]).astype(jnp.int32), partner)


def draw_slot_tables(key, part):
    return plan_tables(key)[0]


def draw_partners(key, part):
    return plan_tables(key)[1]


def draw_slot_rows(key, part):
    key = jax.random.fold_in(key, 5)
    first_key, second_key = jax.random.split(key)
    limits = jax.random.randint(first_key, (2, N_DP * SLOTS), (CAP + 1) // 2, CAP + 1).astype(jnp.int32)
    spot = jax.random.randint(second_key, (2,), 0, N_DP * SLOTS).astype(jnp.int32)
    where_full = jnp.arange(N_DP * SLOTS, dtype=jnp.int32)[None, :] == spot[:, None]
    limits = jnp.where(where_full, CAP, limits)
    return limits.reshape(2, N_DP, SLOTS).astype(jnp.int32)


def place_ends(entries, key, low, high):
    shape = entries.shape
    spot = [jax.random.randint(jax.random.fold_in(key, axis), (), 0, shape[axis]) for axis in range(len(shape))]
    entries = entries.at[tuple(spot)].set(low)
    longest = shape.index(max(shape))
    spot[longest] = (spot[longest] + 1) % shape[longest]
    return entries.at[tuple(spot)].set(high)


def level_of(stream_key, dims, shards, low, largest):
    factor_of = 1.0
    for position, blocks in shards:
        heights = jax.random.uniform(jax.random.fold_in(jax.random.fold_in(stream_key, 6), position), (blocks,), jnp.float32, low / len(shards), largest / len(shards))
        factor_of = factor_of * jnp.repeat(jnp.exp(heights), dims[position] // blocks).reshape((-1,) + (1,) * (len(dims) - 1 - position))
    return factor_of


def deal_out(rng, own, number, rows, count, top, reach, slope):
    order = jax.random.permutation(rng, count)
    heavy_load, common = portions_of(count, rows * top, reach, slope, True), portions_of(count, rows * top, reach, slope, False)
    places = jnp.arange(count)

    def named(tallies, turn):
        used = int((tallies > 0).sum())
        fixed = max(1, used // 4)
        passed = fixed + (places - fixed + turn * (used - fixed)) % max(1, count - fixed)
        return jnp.zeros((count,), jnp.int32).at[order[jnp.where(places < fixed, places, passed)]].set(jnp.asarray(tallies, jnp.int32))

    tallies = jnp.where(number % 4 == 0, named(heavy_load, number // 4), named(common, number - number // 4 - 1))
    mixed = jax.random.permutation(jax.random.fold_in(own, 3), count)
    source_of, receiver = mixed[0:count // 2 * 2:2], mixed[1:count // 2 * 2:2]
    margin = jnp.minimum(tallies[source_of] - 1, reach - tallies[receiver]) // 2
    margin = jnp.where((source_of == order[0]) | (receiver == order[0]) | (tallies[receiver] == 0), 0, jnp.maximum(margin, 0))
    passed = jax.random.randint(jax.random.fold_in(own, 4), (count // 2,), 0, 1 << 20) % (margin + 1)
    tallies = tallies.at[source_of].add(-passed).at[receiver].add(passed)
    items = jnp.searchsorted(jnp.cumsum(tallies), jnp.arange(rows * top), side="right").astype(jnp.int32)
    grid = items.reshape(top, rows).T
    grid = grid[jax.random.permutation(jax.random.fold_in(own, 1), rows)]
    turn = jax.random.randint(jax.random.fold_in(own, 2), (rows, 1), 0, top)
    return jnp.take_along_axis(grid, (jnp.arange(top)[None, :] + turn) % top, axis=1)


def portions_of(amount, total, bound, skew, full):
    loads = [(1 << 20) // math.isqrt(grade ** skew) + 1 for grade in range(1, amount + 1)]
    largest = bound if full else min(bound, max(-(-total // amount), total * loads[0] // sum(loads)))
    least = 1 if total - largest >= amount - 1 else 0
    counts, rest = [largest] + [least] * (amount - 1), total - largest - least * (amount - 1)
    while rest > 0:
        free = [i for i in range(1, amount) if counts[i] < largest] or [i for i in range(1, amount) if counts[i] < bound]
        mass, remaining = sum([loads[i] for i in free]), rest
        for i in free:
            addition = min(bound - counts[i], max(1, remaining * loads[i] // mass), rest)
            counts[i] = counts[i] + addition
            rest = rest - addition
    return np.array(counts)


def normal_values(stream_key, shape, width, most, cuts=(), held_as=jnp.bfloat16):
    drawn = width * jax.random.normal(stream_key, shape, jnp.float32)
    if cuts:
        drawn = drawn * level_of(stream_key, shape, cuts, -0.22, 0.18)
    return jnp.clip(drawn, -most, most).astype(held_as)


def setup_inputs(seed: int = 0) -> dict:
    seeds = jax.random.split(jax.random.key(seed), 11)
    tokens = normal_values(seeds[0], (2, TOKENS, D), 1.0, 6.0, ((1, 512),))
    experts_keys = jax.random.split(jax.random.fold_in(seeds[1], 1), 2 * TOKENS // TOK_DEV)
    experts_turns = jax.random.permutation(jax.random.fold_in(seeds[1], 3), 2 * TOKENS // TOK_DEV)
    experts = jax.vmap(lambda own, number: deal_out(jax.random.fold_in(seeds[1], 2), own, number, TOK_DEV, EXPERTS, TOP, MOST, 2))(experts_keys, experts_turns).reshape((2, TOKENS, TOP))
    replicas = place_ends(jax.random.randint(seeds[2], (2, TOKENS, TOP), 0, 2), jax.random.fold_in(seeds[2], 1), 0, 1).astype(jnp.int32)
    route_weights = jnp.clip(0.1 + 0.4 * jax.random.uniform(seeds[3], (2, TOKENS, TOP), jnp.float32) ** level_of(seeds[3], (2, TOKENS, TOP), ((1, 512),), -0.2, 0.2), 0.1, 0.5)
    slot_tables = draw_slot_tables(jax.random.fold_in(seeds[10], 71), 0)
    partners = draw_partners(jax.random.fold_in(seeds[10], 71), 0)
    slot_rows = draw_slot_rows(jax.random.fold_in(seeds[10], 71), 0)
    gate_w = normal_values(seeds[7], (SLOTS, D, HID), D ** -0.5, 0.09375, ((0, 64), (2, 8)))
    up_w = normal_values(seeds[8], (SLOTS, D, HID), D ** -0.5, 0.09375, ((0, 64), (2, 8)))
    down_w = normal_values(seeds[9], (SLOTS, HID, D), HID ** -0.5, 0.1875, ((0, 64), (2, 8)))
    return {"tokens": tokens, "experts": experts, "replicas": replicas, "route_weights": route_weights, "slot_tables": slot_tables, "partners": partners, "slot_rows": slot_rows, "gate_w": gate_w, "up_w": up_w, "down_w": down_w}


def expert(rows, w_gate, w_up, w_down):
    gate = jnp.dot(rows, w_gate, preferred_element_type=jnp.float32)
    up = jnp.dot(rows, w_up, preferred_element_type=jnp.float32)
    hidden = (jax.nn.silu(gate) * up).astype(jnp.bfloat16)
    return jnp.dot(hidden, w_down, preferred_element_type=jnp.float32).astype(jnp.bfloat16)


def reference(tokens, experts, replicas, route_weights, slot_tables, partners, slot_rows, gate_w, up_w, down_w):
    results = []
    for step in range(2):
        table = slot_tables[step]
        chosen_ids = experts[step]
        slots = jnp.where(replicas[step] == 0, table[chosen_ids, 0], table[chosen_ids, 1]).astype(jnp.int32)
        if step == 0:
            source = jnp.arange(SLOTS, dtype=jnp.int32)
        else:
            source = partners.astype(jnp.int32)
        grouped = slots.reshape(N_DP, -1)
        onehot = (grouped[:, :, None] == jnp.arange(SLOTS, dtype=jnp.int32)[None, None, :]).astype(jnp.int32)
        rank = jnp.sum((jnp.cumsum(onehot, axis=1) - onehot) * onehot, axis=2)
        limit = jnp.take_along_axis(slot_rows[step], grouped, axis=1)
        kept = (rank < limit).reshape(-1)
        flat_slots = slots.reshape(-1)
        gates = route_weights[step].reshape(-1)
        rows_all = tokens[step]

        def visit(total, slot):
            picked = jnp.logical_and(kept, flat_slots == slot)
            index = jnp.nonzero(picked, size=N_DP * CAP, fill_value=0)[0].astype(jnp.int32)
            live = jnp.arange(N_DP * CAP, dtype=jnp.int32) < jnp.sum(picked.astype(jnp.int32))
            owner = (index // TOP).astype(jnp.int32)
            block = source[slot]
            values = expert(rows_all[owner], gate_w[block], up_w[block], down_w[block])
            scale = jnp.where(live, gates[index], jnp.zeros_like(gates[index]))
            term = values.astype(jnp.float32) * scale[:, None]
            return total.at[owner].add(term), None

        total, _ = lax.scan(visit, jnp.zeros((TOKENS, D), jnp.float32), jnp.arange(SLOTS, dtype=jnp.int32))
        results.append(total.astype(jnp.bfloat16))
    return jnp.stack(results)
```

```python
import jax
import jax.numpy as jnp
from jax import lax
from jax.sharding import Mesh, PartitionSpec as P

BF = jnp.bfloat16
F32 = jnp.float32
LANES = 128
ROWS = 48
HOME, HI, MID, ONE, POS = 0, 8, 16, 32, 33


def split_gates(gates):
    high = lax.reduce_precision(gates, 8, 7)
    mid = lax.reduce_precision(gates - high, 8, 7)
    return high.astype(BF), mid.astype(BF)


def pack_meta(experts, replicas, gates, table):
    labels = jnp.arange(table.shape[0], dtype=jnp.int32)
    hot = experts[..., None] == labels
    picked = jnp.where(replicas[..., None] == 0, table[:, 0], table[:, 1])
    home = jnp.sum(jnp.where(hot, picked, 0), axis=-1)
    high, mid = split_gates(gates)
    one = jnp.ones(home.shape, BF)
    meta = jnp.concatenate([home.astype(BF), high, mid, one, one], axis=-1)
    return jnp.pad(meta, ((0, 0), (0, LANES - meta.shape[-1])))


def match_columns(home, me, columns):
    labels = jnp.arange(columns, dtype=jnp.int32) * 4 + me
    return home[..., None] == labels


def occurrence(match, axis):
    count = match.astype(jnp.int32)
    return jnp.cumsum(count, axis=axis) - count


def send_places(home, me, columns, most):
    match = jnp.any(match_columns(home, me, columns), axis=-2)
    earlier = occurrence(match, -2)
    return match[..., None] & (earlier[..., None] == jnp.arange(most, dtype=jnp.int32))


def on_device(
    tokens, experts, replicas, route_weights, slot_tables, partners, slot_rows, gate_w, up_w, down_w
):
    steps, tok, model = tokens.shape
    top = experts.shape[-1]
    n_dp = lax.axis_size("dp")
    columns = lax.axis_size("x") * lax.axis_size("y")
    quad = lax.axis_size("zh") * lax.axis_size("core")
    most = 2
    me = lax.axis_index("zh") * lax.axis_size("core") + lax.axis_index("core")
    column = lax.axis_index("x") * lax.axis_size("y") + lax.axis_index("y")
    my_home = column * quad + me
    my_dp = lax.axis_index("dp")
    mine = steps * tok
    group = quad * mine
    boxes = quad * steps * most
    width = down_w.shape[2]

    meta = pack_meta(
        experts.reshape(mine, top),
        replicas.reshape(mine, top),
        route_weights.reshape(mine, top),
        slot_tables[0],
    )
    packed = jnp.concatenate([tokens.reshape(mine, model), meta], axis=1)
    held = lax.all_gather(packed, ("zh", "core"), axis=0, tiled=True)

    held_meta = held[:, model:]
    home = held_meta[:, HOME : HOME + top].astype(jnp.int32).reshape(quad, steps, tok, top)
    place = send_places(home, me, columns, most)
    same_q = jnp.eye(quad, dtype=jnp.bool_)
    same_u = jnp.eye(steps, dtype=jnp.bool_)
    sender = (
        place.transpose(3, 0, 1, 4, 2)[:, :, :, :, None, None, :]
        & same_q[None, :, None, None, :, None, None]
        & same_u[None, None, :, None, None, :, None]
    ).reshape(columns * boxes, group)
    buffer = jnp.dot(sender.astype(BF), held, preferred_element_type=F32).astype(BF)
    arrived = lax.all_to_all(
        buffer.reshape(columns, boxes, model + LANES),
        ("x", "y"),
        split_axis=0,
        concat_axis=0,
        tiled=True,
    ).reshape(columns * boxes, model + LANES)

    valid = (arrived[:, model + ONE] > 0).reshape(columns, quad, steps, most)
    order = valid.transpose(2, 0, 1, 3).reshape(steps, columns * quad * most)
    rank = occurrence(order, 1)
    labels = jnp.arange(partners.shape[0], dtype=jnp.int32)
    partner_me = jnp.sum(jnp.where(labels == my_home, partners, 0))
    owner = jnp.stack([my_home, partner_me])
    which = (jnp.arange(n_dp, dtype=jnp.int32)[None, :, None] == my_dp) & (
        labels[None, None, :] == owner[:, None, None]
    )
    limit = jnp.sum(jnp.where(which, slot_rows, 0), axis=(1, 2))
    kept = order & (rank < limit[:, None])
    spot = jnp.where(kept, rank + ROWS * jnp.arange(steps, dtype=jnp.int32)[:, None], -1)
    spot = spot.reshape(steps, columns, quad, most).transpose(1, 2, 0, 3).reshape(-1)
    capacity = steps * ROWS
    pick = (spot[None, :] == jnp.arange(capacity, dtype=jnp.int32)[:, None]).astype(BF)
    compact = jnp.dot(pick, arrived[:, :model], preferred_element_type=F32).astype(BF)
    where_from = jnp.dot(
        pick,
        jnp.stack([jnp.arange(columns * boxes), jnp.ones(columns * boxes)], axis=1).astype(BF),
        preferred_element_type=F32,
    )
    position = jnp.where(where_from[:, 1] > 0, where_from[:, 0], -1.0).astype(BF)
    side = jnp.pad(held_meta, ((0, capacity - group), (0, 0)))
    side = jnp.where(
        jnp.arange(LANES, dtype=jnp.int32)[None, :] == POS, position[:, None], side
    )
    rows = lax.all_gather(jnp.concatenate([compact, side], axis=1), "dp", axis=0, tiled=True)

    sides = rows[:, model:].reshape(n_dp, capacity, LANES)
    x = rows[:, :model]
    gate = jnp.dot(x, gate_w[0], preferred_element_type=F32)
    up = jnp.dot(x, up_w[0], preferred_element_type=F32)
    hidden = (jax.nn.silu(gate) * up).astype(BF)
    hiddens = lax.all_gather(hidden, "dp", axis=0, tiled=False)
    output = jnp.einsum(
        "zrh,zhf->rf",
        hiddens,
        down_w[0].reshape(n_dp, hidden.shape[1], width),
        preferred_element_type=F32,
    ).astype(BF)

    positions = sides[:, :, POS].astype(jnp.int32)
    unpick = (
        jnp.arange(columns * boxes, dtype=jnp.int32)[None, :, None] == positions[:, None, :]
    ).astype(BF)
    spread = jnp.einsum(
        "dpc,dcf->dpf",
        unpick,
        output.reshape(n_dp, capacity, width),
        preferred_element_type=F32,
    ).astype(BF)
    back = lax.all_to_all(
        spread.reshape(n_dp, columns, boxes, width).transpose(1, 0, 2, 3),
        ("x", "y"),
        split_axis=0,
        concat_axis=0,
        tiled=True,
    )

    token_meta = sides[:, :group]
    homes = token_meta[..., HOME : HOME + top].astype(jnp.int32).reshape(
        n_dp, quad, steps, tok, top
    )
    hit = match_columns(homes, me, columns)
    places = send_places(homes, me, columns, most)
    parts = []
    for lane in (HI, MID):
        scale = token_meta[..., lane : lane + top].astype(F32).reshape(homes.shape)
        by_column = jnp.sum(jnp.where(hit, scale[..., None], 0.0), axis=-2)
        weight = jnp.where(places, by_column[..., None], 0.0)
        weight = jnp.where(
            same_q[None, :, None, None, None, :, None, None]
            & same_u[None, None, :, None, None, None, :, None],
            weight[:, :, :, :, :, None, None, :],
            0.0,
        )
        parts.append(weight.reshape(n_dp, group, columns * boxes).astype(BF))
    weights = jnp.concatenate(parts, axis=1)
    sums = jnp.einsum(
        "dtp,dpf->dtf",
        weights,
        back.transpose(1, 0, 2, 3).reshape(n_dp, columns * boxes, width),
        preferred_element_type=F32,
    )
    partial = (sums[:, :group] + sums[:, group:]).astype(BF)
    partial = partial.reshape(n_dp, 2, 2, mine, width)
    swapped = lax.all_to_all(
        partial.transpose(2, 1, 0, 3, 4), "core", split_axis=0, concat_axis=0, tiled=True
    )
    halves = jnp.sum(swapped.astype(F32), axis=0).astype(BF)
    pieces = lax.all_to_all(
        halves.reshape(2 * n_dp, mine, width),
        ("zh", "dp"),
        split_axis=0,
        concat_axis=0,
        tiled=True,
    ).reshape(2, n_dp, mine, width)
    mixed = jnp.sum(pieces.astype(F32), axis=0).astype(BF)
    return mixed.transpose(1, 0, 2).reshape(steps, tok, model)


def solution(mesh):
    names = ("dp", "x", "y", "zh", "core")
    grid = Mesh(mesh.devices.reshape(mesh.shape["dp"], 4, 4, 2, 2), names)
    ep = ("x", "y", "zh", "core")
    rows = P(None, names, None)
    return jax.shard_map(
        on_device,
        mesh=grid,
        in_specs=(
            rows,
            rows,
            rows,
            rows,
            P(),
            P(),
            P(),
            P(ep, None, "dp"),
            P(ep, None, "dp"),
            P(ep, None, "dp"),
        ),
        out_specs=rows,
        check_vma=False,
    )
```

```python
import jax
import jax.numpy as jnp
from jax import lax
from jax.sharding import Mesh, PartitionSpec as P

BF = jnp.bfloat16
F32 = jnp.float32
LANES = 128
ROWS = 48
MOST = 2
HOME, HI, MID, ONE, POS = 0, 8, 16, 32, 33


def split_gates(gates):
    high = lax.reduce_precision(gates, 8, 7)
    mid = lax.reduce_precision(gates - high, 8, 7)
    return high.astype(BF), mid.astype(BF)


def pack_meta(experts, replicas, gates, table):
    labels = jnp.arange(table.shape[0], dtype=jnp.int32)
    hot = experts[..., None] == labels
    picked = jnp.where(replicas[..., None] == 0, table[:, 0], table[:, 1])
    home = jnp.sum(jnp.where(hot, picked, 0), axis=-1)
    high, mid = split_gates(gates)
    one = jnp.ones(home.shape, BF)
    meta = jnp.concatenate([home.astype(BF), high, mid, one, one], axis=-1)
    return jnp.pad(meta, ((0, 0), (0, LANES - meta.shape[-1])))


def places(meta, me, columns, quad, tok, top):
    n = meta.shape[0]
    box = jnp.arange(columns * quad * MOST, dtype=jnp.int32)[None, :]
    row = jnp.arange(n, dtype=jnp.int32)[:, None]
    target = (box // (quad * MOST) * quad + me).astype(BF)
    same = (row // tok) % quad == (box // MOST) % quad
    hits = [(meta[:, HOME + k : HOME + k + 1] == target) & same for k in range(top)]
    match = hits[0]
    for hit in hits[1:]:
        match = match | hit
    other = jnp.arange(n, dtype=jnp.int32)[None, :]
    before = ((row // tok == other // tok) & (other < row)).astype(BF)
    earlier = jnp.dot(before, match.astype(BF), preferred_element_type=F32)
    return hits, match & (earlier == (box % MOST).astype(F32))


def on_device(
    tokens, experts, replicas, route_weights, slot_tables, partners, slot_rows, gate_w, up_w, down_w
):
    steps, tok, model = tokens.shape
    top = experts.shape[-1]
    n_dp = lax.axis_size("dp")
    columns = lax.axis_size("x") * lax.axis_size("y")
    quad = lax.axis_size("zh") * lax.axis_size("core")
    me = lax.axis_index("zh") * lax.axis_size("core") + lax.axis_index("core")
    column = lax.axis_index("x") * lax.axis_size("y") + lax.axis_index("y")
    my_home = column * quad + me
    my_dp = lax.axis_index("dp")
    mine = steps * tok
    group = quad * tok
    boxes = columns * quad * MOST
    wide = model + LANES
    width = down_w.shape[2]

    right = [[(i, i + 1) for i in range(j, n_dp - 1)] for j in range(n_dp - 1)]
    left = [[(i + 1, i) for i in range(n_dp - 1 - j)] for j in range(n_dp - 1)]

    meta = pack_meta(
        experts.reshape(mine, top),
        replicas.reshape(mine, top),
        route_weights.reshape(mine, top),
        slot_tables[0],
    )
    packed = jnp.concatenate([tokens.reshape(mine, model), meta], axis=1)
    held = lax.all_gather(packed.reshape(steps, tok, wide), ("zh", "core"), axis=1, tiled=True)

    labels = jnp.arange(partners.shape[0], dtype=jnp.int32)
    partner_me = jnp.sum(jnp.where(labels == my_home, partners, 0))
    owners = (my_home, partner_me)
    lanes = jnp.arange(LANES, dtype=jnp.int32)[None, :]
    line = jnp.arange(boxes, dtype=jnp.int32)
    lower = (line[:, None] < line[None, :]).astype(BF)

    def dispatch(step):
        local = held[step]
        local_meta = local[:, model:]
        place = places(local_meta, me, columns, quad, tok, top)[1]
        buffer = lax.dot_general(
            place.astype(BF), local, (((0,), (0,)), ((), ())), preferred_element_type=F32
        ).astype(BF)
        arrived = lax.all_to_all(
            buffer.reshape(columns, quad * MOST, wide),
            ("x", "y"),
            split_axis=0,
            concat_axis=0,
            tiled=True,
        ).reshape(boxes, wide)
        valid = arrived[:, model + ONE]
        rank = jnp.dot(valid[None, :], lower, preferred_element_type=F32)
        which = (jnp.arange(n_dp, dtype=jnp.int32)[:, None] == my_dp) & (
            labels[None, :] == owners[step]
        )
        limit = jnp.sum(jnp.where(which, slot_rows[step], 0)).astype(F32)
        kept = (valid[None, :] > 0) & (rank < limit)
        slot_row = jnp.arange(ROWS, dtype=jnp.int32).astype(F32)[:, None]
        chosen = kept & (rank == slot_row)
        pick = chosen.astype(BF)
        compact = jnp.dot(pick, arrived[:, :model], preferred_element_type=F32).astype(BF)
        position = jnp.sum(
            jnp.where(chosen, line.astype(F32)[None, :] + 1.0, 0.0), axis=1, keepdims=True
        )
        side = jnp.pad(local_meta, ((0, ROWS - group), (0, 0)))
        side = jnp.where(lanes == POS, position.astype(BF), side)
        return jnp.concatenate([compact, side], axis=1)

    def project(block):
        x = block[:, :model]
        gate = jnp.dot(x, gate_w[0], preferred_element_type=F32)
        up = jnp.dot(x, up_w[0], preferred_element_type=F32)
        hidden = (jax.nn.silu(gate) * up).astype(BF)
        return jnp.concatenate([hidden, block[:, model:]], axis=1)

    own = [dispatch(step) for step in range(steps)]
    by_offset = [[project(block)] + [None] * (n_dp - 1) for block in own]
    to_right, to_left = list(own), list(own)
    from_left = [[None] * n_dp for _ in range(steps)]
    from_right = [[None] * n_dp for _ in range(steps)]
    for j in range(n_dp - 1):
        for s in range(steps):
            to_right[s] = lax.ppermute(to_right[s], "dp", right[j])
            to_left[s] = lax.ppermute(to_left[s], "dp", left[j])
            both = project(jnp.concatenate([to_right[s], to_left[s]], axis=0))
            from_left[s][j + 1], from_right[s][j + 1] = both[:ROWS], both[ROWS:]
    for s in range(steps):
        for m in range(1, n_dp):
            by_offset[s][m] = from_right[s][m] + from_left[s][n_dp - m]
    ordered = jnp.stack([jnp.stack(blocks) for blocks in by_offset], axis=1)
    ordered = lax.dynamic_slice_in_dim(
        jnp.concatenate([ordered, ordered], axis=0), n_dp - my_dp, n_dp, axis=0
    )
    batch = n_dp * steps
    hidden = ordered[..., :LANES].reshape(batch * ROWS, LANES)
    sides = ordered[..., LANES:].reshape(batch, ROWS, LANES)

    down = down_w[0].reshape(n_dp, LANES, width)

    def shard(index):
        return lax.dynamic_index_in_dim(down, lax.rem(index + n_dp, n_dp), 0, keepdims=False)

    total = jnp.dot(hidden, shard(my_dp), preferred_element_type=F32)
    going_right, going_left = hidden, hidden
    for j in range(n_dp - 1):
        going_right = lax.ppermute(going_right, "dp", right[j])
        going_left = lax.ppermute(going_left, "dp", left[j])
        total = total + jnp.dot(
            jnp.concatenate([going_right, going_left], axis=1),
            jnp.concatenate([shard(my_dp - j - 1), shard(my_dp + j + 1)], axis=0),
            preferred_element_type=F32,
        )
    output = total.astype(BF)

    positions = sides[:, :, POS].astype(jnp.int32) - 1
    unpick = (line[None, :, None] == positions[:, None, :]).astype(BF)
    spread = jnp.einsum(
        "bpr,brf->bpf",
        unpick,
        output.reshape(batch, ROWS, width),
        preferred_element_type=F32,
    ).astype(BF)
    back = lax.all_to_all(
        spread.reshape(batch, columns, quad * MOST, width).transpose(1, 0, 2, 3),
        ("x", "y"),
        split_axis=0,
        concat_axis=0,
        tiled=True,
    )

    token_meta = sides[:, :group].reshape(batch * group, LANES)
    hits, place = places(token_meta, me, columns, quad, tok, top)
    parts = []
    for lane in (HI, MID):
        weight = jnp.zeros((batch * group, boxes), F32)
        for k in range(top):
            weight = jnp.where(
                hits[k], token_meta[:, lane + k : lane + k + 1].astype(F32), weight
            )
        parts.append(jnp.where(place, weight, 0.0).astype(BF).reshape(batch, group, boxes))
    sums = jnp.einsum(
        "btp,bpf->btf",
        jnp.concatenate(parts, axis=1),
        back.transpose(1, 0, 2, 3).reshape(batch, boxes, width),
        preferred_element_type=F32,
    )
    partial = (sums[:, :group] + sums[:, group:]).astype(BF)
    partial = partial.reshape(n_dp, steps, 2, 2, tok, width).transpose(3, 2, 0, 1, 4, 5)
    swapped = lax.all_to_all(partial, "core", split_axis=0, concat_axis=0, tiled=True)
    halves = jnp.sum(swapped.astype(F32), axis=0).astype(BF)
    pieces = lax.all_to_all(
        halves.reshape(2 * n_dp, mine, width),
        ("zh", "dp"),
        split_axis=0,
        concat_axis=0,
        tiled=True,
    ).reshape(2, n_dp, mine, width)
    mixed = jnp.sum(pieces.astype(F32), axis=0).astype(BF)
    return mixed.transpose(1, 0, 2).reshape(steps, tok, model)


def solution(mesh):
    names = ("dp", "x", "y", "zh", "core")
    grid = Mesh(mesh.devices.reshape(mesh.shape["dp"], 4, 4, 2, 2), names)
    ep = ("x", "y", "zh", "core")
    rows = P(None, names, None)
    return jax.shard_map(
        on_device,
        mesh=grid,
        in_specs=(
            rows,
            rows,
            rows,
            rows,
            P(),
            P(),
            P(),
            P(ep, None, "dp"),
            P(ep, None, "dp"),
            P(ep, None, "dp"),
        ),
        out_specs=rows,
        check_vma=False,
    )
```

```python
import jax
import jax.numpy as jnp
from jax import lax
from jax.sharding import Mesh, PartitionSpec as P

BF = jnp.bfloat16
F32 = jnp.float32
LANES = 128
ROWS = 48
MOST = 2
HOME, HI, MID, ONE, POS = 0, 8, 16, 32, 33


def split_gates(gates):
    high = lax.reduce_precision(gates, 8, 7)
    mid = lax.reduce_precision(gates - high, 8, 7)
    return high.astype(BF), mid.astype(BF)


def pack_meta(experts, replicas, gates, table):
    labels = jnp.arange(table.shape[0], dtype=jnp.int32)
    hot = experts[..., None] == labels
    picked = jnp.where(replicas[..., None] == 0, table[:, 0], table[:, 1])
    home = jnp.sum(jnp.where(hot, picked, 0), axis=-1)
    high, mid = split_gates(gates)
    one = jnp.ones(home.shape, BF)
    meta = jnp.concatenate([home.astype(BF), high, mid, one, one], axis=-1)
    return jnp.pad(meta, ((0, 0), (0, LANES - meta.shape[-1])))


def places(meta, me, columns, quad, tok, top):
    n = meta.shape[0]
    box = jnp.arange(columns * quad * MOST, dtype=jnp.int32)[None, :]
    row = jnp.arange(n, dtype=jnp.int32)[:, None]
    target = (box // (quad * MOST) * quad + me).astype(BF)
    same = (row // tok) % quad == (box // MOST) % quad
    hits = [(meta[:, HOME + k : HOME + k + 1] == target) & same for k in range(top)]
    match = hits[0]
    for hit in hits[1:]:
        match = match | hit
    other = jnp.arange(n, dtype=jnp.int32)[None, :]
    before = ((row // tok == other // tok) & (other < row)).astype(BF)
    earlier = jnp.dot(before, match.astype(BF), preferred_element_type=F32)
    return hits, match & (earlier == (box % MOST).astype(F32))


def on_device(
    tokens, experts, replicas, route_weights, slot_tables, partners, slot_rows, gate_w, up_w, down_w
):
    steps, tok, model = tokens.shape
    top = experts.shape[-1]
    n_dp = lax.axis_size("dp")
    columns = lax.axis_size("x") * lax.axis_size("y")
    quad = lax.axis_size("zh") * lax.axis_size("core")
    me = lax.axis_index("zh") * lax.axis_size("core") + lax.axis_index("core")
    column = lax.axis_index("x") * lax.axis_size("y") + lax.axis_index("y")
    my_home = column * quad + me
    my_dp = lax.axis_index("dp")
    mine = steps * tok
    group = quad * tok
    boxes = columns * quad * MOST
    wide = model + LANES
    width = down_w.shape[2]

    right = [[(i, i + 1) for i in range(j, n_dp - 1)] for j in range(n_dp - 1)]
    left = [[(i + 1, i) for i in range(n_dp - 1 - j)] for j in range(n_dp - 1)]

    meta = pack_meta(
        experts.reshape(mine, top),
        replicas.reshape(mine, top),
        route_weights.reshape(mine, top),
        slot_tables[0],
    )
    packed = jnp.concatenate([tokens.reshape(mine, model), meta], axis=1)
    held = lax.all_gather(packed.reshape(steps, tok, wide), ("zh", "core"), axis=1, tiled=True)

    labels = jnp.arange(partners.shape[0], dtype=jnp.int32)
    partner_me = jnp.sum(jnp.where(labels == my_home, partners, 0))
    owners = (my_home, partner_me)
    lanes = jnp.arange(LANES, dtype=jnp.int32)[None, :]
    line = jnp.arange(boxes, dtype=jnp.int32)
    lower = (line[:, None] < line[None, :]).astype(BF)

    send = []
    for step in range(steps):
        local = held[step]
        place = places(local[:, model:], me, columns, quad, tok, top)[1]
        send.append(
            lax.dot_general(
                place.astype(BF), local, (((0,), (0,)), ((), ())), preferred_element_type=F32
            )
            .astype(BF)
            .reshape(columns, quad * MOST, wide)
        )
    received = lax.all_to_all(
        jnp.concatenate(send, axis=1), ("x", "y"), split_axis=0, concat_axis=0, tiled=True
    )

    def compacted(step):
        arrived = received[:, step * quad * MOST : (step + 1) * quad * MOST].reshape(boxes, wide)
        valid = arrived[:, model + ONE]
        rank = jnp.dot(valid[None, :], lower, preferred_element_type=F32)
        which = (jnp.arange(n_dp, dtype=jnp.int32)[:, None] == my_dp) & (
            labels[None, :] == owners[step]
        )
        limit = jnp.sum(jnp.where(which, slot_rows[step], 0)).astype(F32)
        kept = (valid[None, :] > 0) & (rank < limit)
        slot_row = jnp.arange(ROWS, dtype=jnp.int32).astype(F32)[:, None]
        chosen = kept & (rank == slot_row)
        pick = chosen.astype(BF)
        compact = jnp.dot(pick, arrived[:, :model], preferred_element_type=F32).astype(BF)
        position = jnp.sum(
            jnp.where(chosen, line.astype(F32)[None, :] + 1.0, 0.0), axis=1, keepdims=True
        )
        side = jnp.pad(held[step][:, model:], ((0, ROWS - group), (0, 0)))
        side = jnp.where(lanes == POS, position.astype(BF), side)
        return jnp.concatenate([compact, side], axis=1)

    def project(block):
        x = block[:, :model]
        gate = jnp.dot(x, gate_w[0], preferred_element_type=F32)
        up = jnp.dot(x, up_w[0], preferred_element_type=F32)
        hidden = (jax.nn.silu(gate) * up).astype(BF)
        return jnp.concatenate([hidden, block[:, model:]], axis=1)

    def ring(chunks):
        to_right, to_left = list(chunks), list(chunks)
        from_left = [[None] * n_dp for _ in chunks]
        from_right = [[None] * n_dp for _ in chunks]
        for j in range(n_dp - 1):
            for s in range(len(chunks)):
                to_right[s] = lax.ppermute(to_right[s], "dp", right[j])
                to_left[s] = lax.ppermute(to_left[s], "dp", left[j])
                from_left[s][j + 1], from_right[s][n_dp - 1 - j] = to_right[s], to_left[s]
        return [
            [own] + [a + b for a, b in zip(from_left[s][1:], from_right[s][1:])]
            for s, own in enumerate(chunks)
        ]

    early = [m for m in range(n_dp) if m not in (1, n_dp - 1)]
    late = [1, n_dp - 1]
    ordered = []
    for slots in ring([compacted(step) for step in range(steps)]):
        blocks = [None] * n_dp
        for some in (early, late):
            done = project(jnp.concatenate([slots[m] for m in some], axis=0))
            for i, m in enumerate(some):
                blocks[-m % n_dp] = done[i * ROWS : (i + 1) * ROWS]
        twice = jnp.stack(blocks + blocks)
        ordered.append(lax.dynamic_slice_in_dim(twice, n_dp - my_dp, n_dp, axis=0))
    batch = steps * n_dp
    hidden = [one[..., :LANES].reshape(n_dp * ROWS, LANES) for one in ordered]
    sides = jnp.concatenate([one[..., LANES:] for one in ordered], axis=0)

    down = down_w[0].reshape(n_dp, LANES, width)
    down = [
        lax.dynamic_index_in_dim(down, lax.rem(my_dp - m + n_dp, n_dp), 0, keepdims=False)
        for m in range(n_dp)
    ]
    output = []
    for slots in ring(hidden):
        sums = [
            jnp.dot(
                jnp.concatenate([slots[m] for m in some], axis=1),
                jnp.concatenate([down[m] for m in some], axis=0),
                preferred_element_type=F32,
            )
            for some in (early, late)
        ]
        output.append(sums[0] + sums[1])
    output = jnp.stack(output).astype(BF)

    positions = sides[:, :, POS].astype(jnp.int32) - 1
    unpick = (line[None, :, None] == positions[:, None, :]).astype(BF)
    spread = jnp.einsum(
        "bpr,brf->bpf",
        unpick,
        output.reshape(batch, ROWS, width),
        preferred_element_type=F32,
    ).astype(BF)
    back = lax.all_to_all(
        spread.reshape(batch, columns, quad * MOST, width).transpose(1, 0, 2, 3),
        ("x", "y"),
        split_axis=0,
        concat_axis=0,
        tiled=True,
    )

    token_meta = sides[:, :group].reshape(batch * group, LANES)
    hits, place = places(token_meta, me, columns, quad, tok, top)
    parts = []
    for lane in (HI, MID):
        weight = jnp.zeros((batch * group, boxes), F32)
        for k in range(top):
            weight = jnp.where(
                hits[k], token_meta[:, lane + k : lane + k + 1].astype(F32), weight
            )
        parts.append(jnp.where(place, weight, 0.0).astype(BF).reshape(batch, group, boxes))
    sums = jnp.einsum(
        "btp,bpf->btf",
        jnp.concatenate(parts, axis=1),
        back.transpose(1, 0, 2, 3).reshape(batch, boxes, width),
        preferred_element_type=F32,
    )
    partial = (sums[:, :group] + sums[:, group:]).astype(BF)
    partial = partial.reshape(steps, n_dp, 2, 2, tok, width).transpose(3, 2, 1, 0, 4, 5)
    swapped = lax.all_to_all(partial, "core", split_axis=0, concat_axis=0, tiled=True)
    halves = jnp.sum(swapped.astype(F32), axis=0).astype(BF)
    pieces = lax.all_to_all(
        halves.reshape(2 * n_dp, mine * width // LANES, LANES),
        ("zh", "dp"),
        split_axis=0,
        concat_axis=0,
        tiled=True,
    ).reshape(2, n_dp, mine, width)
    mixed = jnp.sum(pieces.astype(F32), axis=0).astype(BF)
    return mixed.transpose(1, 0, 2).reshape(steps, tok, model)


def solution(mesh):
    names = ("dp", "x", "y", "zh", "core")
    grid = Mesh(mesh.devices.reshape(mesh.shape["dp"], 4, 4, 2, 2), names)
    ep = ("x", "y", "zh", "core")
    rows = P(None, names, None)
    return jax.shard_map(
        on_device,
        mesh=grid,
        in_specs=(
            rows,
            rows,
            rows,
            rows,
            P(),
            P(),
            P(),
            P(ep, None, "dp"),
            P(ep, None, "dp"),
            P(ep, None, "dp"),
        ),
        out_specs=rows,
        check_vma=False,
    )
```

```python
import functools

import jax
import jax.numpy as jnp
from jax import lax
from jax.experimental import pallas as pl
from jax.experimental.pallas import tpu as pltpu
from jax.sharding import Mesh, PartitionSpec as P

BF = jnp.bfloat16
F32 = jnp.float32
LANES = 128
ROWS = 48
MOST = 2
EARLY = 5
HOME, HI, MID, ONE, POS = 0, 8, 16, 32, 33


def split_gates(gates):
    high = lax.reduce_precision(gates, 8, 7)
    mid = lax.reduce_precision(gates - high, 8, 7)
    return high.astype(BF), mid.astype(BF)


def pack_meta(experts, replicas, gates, table):
    labels = jnp.arange(table.shape[0], dtype=jnp.int32)
    hot = experts[..., None] == labels
    picked = jnp.where(replicas[..., None] == 0, table[:, 0], table[:, 1])
    home = jnp.sum(jnp.where(hot, picked, 0), axis=-1)
    high, mid = split_gates(gates)
    one = jnp.ones(home.shape, BF)
    meta = jnp.concatenate([home.astype(BF), high, mid, one, one], axis=-1)
    return jnp.pad(meta, ((0, 0), (0, LANES - meta.shape[-1])))


def places(meta, me, columns, quad, tok, top):
    n = meta.shape[0]
    box = jnp.arange(columns * quad * MOST, dtype=jnp.int32)[None, :]
    row = jnp.arange(n, dtype=jnp.int32)[:, None]
    target = (box // (quad * MOST) * quad + me).astype(BF)
    same = (row // tok) % quad == (box // MOST) % quad
    hits = [(meta[:, HOME + k : HOME + k + 1] == target) & same for k in range(top)]
    match = hits[0]
    for hit in hits[1:]:
        match = match | hit
    other = jnp.arange(n, dtype=jnp.int32)[None, :]
    before = ((row // tok == other // tok) & (other < row)).astype(BF)
    earlier = jnp.dot(before, match.astype(BF), preferred_element_type=F32)
    return hits, match & (earlier == (box % MOST).astype(F32))


def project_kernel(count, passed, extra, weight_ref, *refs):
    blocks = refs[:count]
    outs = refs[count + extra + passed : 2 * count + extra + passed]
    rows_ref, sems = refs[-2:]
    width = weight_ref.shape[1] // 2
    model = weight_ref.shape[0]
    copies = [
        pltpu.make_async_copy(
            blocks[i], rows_ref.at[pl.ds(i * ROWS, ROWS)], sems.at[i]
        )
        for i in range(count)
    ]
    for copy in copies:
        copy.start()
    for copy in copies:
        copy.wait()
    both = jnp.dot(rows_ref[:, :model], weight_ref[...], preferred_element_type=F32)
    gate, up = both[:, :width], both[:, width:]
    hidden = (gate / (1.0 + jnp.exp(-gate)) * up).astype(BF)
    for i in range(count):
        outs[i][:, :width] = hidden[i * ROWS : (i + 1) * ROWS]
        outs[i][:, width:] = rows_ref[i * ROWS : (i + 1) * ROWS, model:]


SMALL = pl.CostEstimate(flops=1000, bytes_accessed=1000, transcendentals=0)


def project(weight, blocks, passed, extra=()):
    vmem = pl.BlockSpec(memory_space=pltpu.VMEM)
    there = pl.BlockSpec(memory_space=pl.ANY)
    count = len(blocks)
    out = pl.pallas_call(
        functools.partial(project_kernel, count, passed, len(extra)),
        out_shape=[jax.ShapeDtypeStruct(block.shape, BF) for block in blocks[:passed]]
        + [jax.ShapeDtypeStruct((ROWS, 2 * LANES), BF)] * count,
        in_specs=[vmem] + [there] * (count + len(extra)),
        out_specs=[there] * passed + [vmem] * count,
        input_output_aliases={1 + i: i for i in range(passed)},
        scratch_shapes=[
            pltpu.VMEM((count * ROWS, blocks[0].shape[1]), BF),
            pltpu.SemaphoreType.DMA((count,)),
        ],
        compiler_params=pltpu.CompilerParams(vmem_limit_bytes=24 * 2**20),
        cost_estimate=SMALL,
    )(weight, *blocks, *extra)
    return out[:passed], out[passed:]


def assemble_kernel(plan, low, n_dp, dp_ref, *refs):
    out_ref = refs[-1]
    z = dp_ref[0]
    for (s, m), members in plan:
        value = refs[members[0]][:, low : low + LANES]
        for other in members[1:]:
            value = value + refs[other][:, low : low + LANES]
        spot = s * n_dp + lax.rem(z - m + n_dp, n_dp)
        out_ref[pl.ds(pl.multiple_of(spot * ROWS, ROWS), ROWS), :] = value


def assemble(done, low, my_dp):
    plan, flat = [], []
    for s, slots in enumerate(done):
        for m, parts in enumerate(slots):
            plan.append(((s, m), tuple(range(len(flat), len(flat) + len(parts)))))
            flat += parts
    n_dp = len(done[0])
    vmem = pl.BlockSpec(memory_space=pltpu.VMEM)
    return pl.pallas_call(
        functools.partial(assemble_kernel, plan, low, n_dp),
        out_shape=jax.ShapeDtypeStruct((len(plan) * ROWS, LANES), BF),
        in_specs=[pl.BlockSpec(memory_space=pltpu.SMEM)] + [vmem] * len(flat),
        out_specs=vmem,
        compiler_params=pltpu.CompilerParams(vmem_limit_bytes=8 * 2**20),
        cost_estimate=SMALL,
    )(my_dp.astype(jnp.int32).reshape(1), *flat)


def on_device(
    tokens, experts, replicas, route_weights, slot_tables, partners, slot_rows, gate_w, up_w, down_w
):
    steps, tok, model = tokens.shape
    top = experts.shape[-1]
    n_dp = lax.axis_size("dp")
    columns = lax.axis_size("x") * lax.axis_size("y")
    quad = lax.axis_size("zh") * lax.axis_size("core")
    me = lax.axis_index("zh") * lax.axis_size("core") + lax.axis_index("core")
    column = lax.axis_index("x") * lax.axis_size("y") + lax.axis_index("y")
    my_home = column * quad + me
    my_dp = lax.axis_index("dp")
    mine = steps * tok
    group = quad * tok
    boxes = columns * quad * MOST
    wide = model + LANES
    width = down_w.shape[2]

    right = [[(i, i + 1) for i in range(j, n_dp - 1)] for j in range(n_dp - 1)]
    left = [[(i + 1, i) for i in range(n_dp - 1 - j)] for j in range(n_dp - 1)]

    meta = pack_meta(
        experts.reshape(mine, top),
        replicas.reshape(mine, top),
        route_weights.reshape(mine, top),
        slot_tables[0],
    )
    packed = jnp.concatenate([tokens.reshape(mine, model), meta], axis=1)
    held = lax.all_gather(packed.reshape(steps, tok, wide), ("zh", "core"), axis=1, tiled=True)

    labels = jnp.arange(partners.shape[0], dtype=jnp.int32)
    partner_me = jnp.sum(jnp.where(labels == my_home, partners, 0))
    owners = (my_home, partner_me)
    lanes = jnp.arange(LANES, dtype=jnp.int32)[None, :]
    line = jnp.arange(boxes, dtype=jnp.int32)
    lower = (line[:, None] < line[None, :]).astype(BF)

    send = []
    for step in range(steps):
        local = held[step]
        place = places(local[:, model:], me, columns, quad, tok, top)[1]
        send.append(
            lax.dot_general(
                place.astype(BF), local, (((0,), (0,)), ((), ())), preferred_element_type=F32
            )
            .astype(BF)
            .reshape(columns, quad * MOST, wide)
        )
    received = lax.all_to_all(
        jnp.concatenate(send, axis=1), ("x", "y"), split_axis=0, concat_axis=0, tiled=True
    )

    def compacted(step):
        arrived = received[:, step * quad * MOST : (step + 1) * quad * MOST].reshape(boxes, wide)
        valid = arrived[:, model + ONE]
        rank = jnp.dot(valid[None, :], lower, preferred_element_type=F32)
        which = (jnp.arange(n_dp, dtype=jnp.int32)[:, None] == my_dp) & (
            labels[None, :] == owners[step]
        )
        limit = jnp.sum(jnp.where(which, slot_rows[step], 0)).astype(F32)
        kept = (valid[None, :] > 0) & (rank < limit)
        slot_row = jnp.arange(ROWS, dtype=jnp.int32).astype(F32)[:, None]
        chosen = kept & (rank == slot_row)
        pick = chosen.astype(BF)
        compact = jnp.dot(pick, arrived[:, :model], preferred_element_type=F32).astype(BF)
        position = jnp.sum(
            jnp.where(chosen, line.astype(F32)[None, :] + 1.0, 0.0), axis=1, keepdims=True
        )
        side = jnp.pad(held[step][:, model:], ((0, ROWS - group), (0, 0)))
        side = jnp.where(lanes == POS, position.astype(BF), side)
        return jnp.concatenate([compact, side], axis=1)

    both_w = jnp.concatenate([gate_w[0], up_w[0]], axis=1)
    batch = steps * n_dp
    own = [compacted(step) for step in range(steps)]
    to_right, to_left = list(own), list(own)
    done = [[[] for _ in range(n_dp)] for _ in range(steps)]
    far = [[None] * n_dp for _ in range(steps)]
    hidden = None
    for j in range(1, n_dp):
        for s in range(steps):
            to_right[s] = lax.ppermute(to_right[s], "dp", right[j - 1])
            to_left[s] = lax.ppermute(to_left[s], "dp", left[j - 1])
            blocks = [to_right[s], to_left[s]] + ([own[s]] if j == 1 else [])
            passed = 2 if j < n_dp - 1 else 0
            extra = [hidden] if j == EARLY + 1 and s == 0 else []
            sent, made = project(both_w, blocks, passed, extra)
            if passed:
                to_right[s], to_left[s] = sent
            if j > EARLY:
                far[s][j] = made[0][:, :LANES] + made[1][:, :LANES]
            done[s][j].append(made[0])
            done[s][n_dp - j].append(made[1])
            if j == 1:
                done[s][0].append(made[2])
        if j == EARLY:
            hidden = assemble(done, 0, my_dp)
    gathered = lax.all_gather(hidden, "dp", axis=0, tiled=False).reshape(
        n_dp, steps, n_dp, ROWS, LANES
    )
    beyond = range(EARLY + 1, n_dp)
    rest = jnp.stack([jnp.stack([far[s][k] for k in beyond]) for s in range(steps)])
    rest = lax.all_to_all(
        jnp.broadcast_to(
            rest.reshape(1, steps * len(beyond) * ROWS, LANES),
            (n_dp, steps * len(beyond) * ROWS, LANES),
        ),
        "dp",
        split_axis=0,
        concat_axis=0,
        tiled=True,
    ).reshape(n_dp, steps, len(beyond), ROWS, LANES)
    for z in range(n_dp):
        for i, k in enumerate(beyond):
            for d in (z - k, z + k):
                if 0 <= d < n_dp:
                    gathered = lax.dynamic_update_slice(
                        gathered, rest[z : z + 1, :, i : i + 1], (z, 0, d, 0, 0)
                    )
    output = jnp.einsum(
        "zrh,zhf->rf",
        gathered.reshape(n_dp, batch * ROWS, LANES),
        down_w[0].reshape(n_dp, LANES, width),
        preferred_element_type=F32,
    ).astype(BF)

    sides = assemble(done, LANES, my_dp).reshape(batch, ROWS, LANES)

    positions = sides[:, :, POS].astype(jnp.int32) - 1
    unpick = (line[None, :, None] == positions[:, None, :]).astype(BF)
    spread = jnp.einsum(
        "bpr,brf->bpf",
        unpick,
        output.reshape(batch, ROWS, width),
        preferred_element_type=F32,
    ).astype(BF)
    back = lax.all_to_all(
        spread.reshape(batch, columns, quad * MOST, width).transpose(1, 0, 2, 3),
        ("x", "y"),
        split_axis=0,
        concat_axis=0,
        tiled=True,
    )

    token_meta = sides[:, :group].reshape(batch * group, LANES)
    hits, place = places(token_meta, me, columns, quad, tok, top)
    parts = []
    for lane in (HI, MID):
        weight = jnp.zeros((batch * group, boxes), F32)
        for k in range(top):
            weight = jnp.where(
                hits[k], token_meta[:, lane + k : lane + k + 1].astype(F32), weight
            )
        parts.append(jnp.where(place, weight, 0.0).astype(BF).reshape(batch, group, boxes))
    sums = jnp.einsum(
        "btp,bpf->btf",
        jnp.concatenate(parts, axis=1),
        back.transpose(1, 0, 2, 3).reshape(batch, boxes, width),
        preferred_element_type=F32,
    )
    partial = (sums[:, :group] + sums[:, group:]).astype(BF)
    partial = partial.reshape(steps, n_dp, 2, 2, tok, width).transpose(3, 2, 1, 0, 4, 5)
    swapped = lax.all_to_all(partial, "core", split_axis=0, concat_axis=0, tiled=True)
    halves = jnp.sum(swapped.astype(F32), axis=0).astype(BF)
    pieces = lax.all_to_all(
        halves.reshape(2 * n_dp, mine * width // LANES, LANES),
        ("zh", "dp"),
        split_axis=0,
        concat_axis=0,
        tiled=True,
    ).reshape(2, n_dp, mine, width)
    mixed = jnp.sum(pieces.astype(F32), axis=0).astype(BF)
    return mixed.transpose(1, 0, 2).reshape(steps, tok, model)


def solution(mesh):
    names = ("dp", "x", "y", "zh", "core")
    grid = Mesh(mesh.devices.reshape(mesh.shape["dp"], 4, 4, 2, 2), names)
    ep = ("x", "y", "zh", "core")
    rows = P(None, names, None)
    return jax.shard_map(
        on_device,
        mesh=grid,
        in_specs=(
            rows,
            rows,
            rows,
            rows,
            P(),
            P(),
            P(),
            P(ep, None, "dp"),
            P(ep, None, "dp"),
            P(ep, None, "dp"),
        ),
        out_specs=rows,
        check_vma=False,
    )
```

```python
import functools

import jax
import jax.numpy as jnp
from jax import lax
from jax.experimental import pallas as pl
from jax.experimental.pallas import tpu as pltpu
from jax.sharding import Mesh, PartitionSpec as P

BF = jnp.bfloat16
F32 = jnp.float32
LANES = 128
ROWS = 48
MOST = 2
EARLY = 3
STEPS = 5
HOME, HI, MID, ONE, POS = 0, 8, 16, 32, 33


def split_gates(gates):
    high = lax.reduce_precision(gates, 8, 7)
    mid = lax.reduce_precision(gates - high, 8, 7)
    return high.astype(BF), mid.astype(BF)


def pack_meta(experts, replicas, gates, table):
    labels = jnp.arange(table.shape[0], dtype=jnp.int32)
    hot = experts[..., None] == labels
    picked = jnp.where(replicas[..., None] == 0, table[:, 0], table[:, 1])
    home = jnp.sum(jnp.where(hot, picked, 0), axis=-1)
    high, mid = split_gates(gates)
    one = jnp.ones(home.shape, BF)
    meta = jnp.concatenate([home.astype(BF), high, mid, one, one], axis=-1)
    return jnp.pad(meta, ((0, 0), (0, LANES - meta.shape[-1])))


def places(meta, me, columns, quad, tok, top):
    n = meta.shape[0]
    box = jnp.arange(columns * quad * MOST, dtype=jnp.int32)[None, :]
    row = jnp.arange(n, dtype=jnp.int32)[:, None]
    target = (box // (quad * MOST) * quad + me).astype(BF)
    same = (row // tok) % quad == (box // MOST) % quad
    hits = [(meta[:, HOME + k : HOME + k + 1] == target) & same for k in range(top)]
    match = hits[0]
    for hit in hits[1:]:
        match = match | hit
    other = jnp.arange(n, dtype=jnp.int32)[None, :]
    before = ((row // tok == other // tok) & (other < row)).astype(BF)
    earlier = jnp.dot(before, match.astype(BF), preferred_element_type=F32)
    return hits, match & (earlier == (box % MOST).astype(F32))


def project_kernel(count, passed, extra, weight_ref, *refs):
    blocks = refs[:count]
    outs = refs[count + extra + passed : 2 * count + extra + passed]
    rows_ref, sems = refs[-2:]
    width = weight_ref.shape[1] // 2
    model = weight_ref.shape[0]
    copies = [
        pltpu.make_async_copy(
            blocks[i], rows_ref.at[pl.ds(i * ROWS, ROWS)], sems.at[i]
        )
        for i in range(count)
    ]
    for copy in copies:
        copy.start()
    for copy in copies:
        copy.wait()
    both = jnp.dot(rows_ref[:, :model], weight_ref[...], preferred_element_type=F32)
    gate, up = both[:, :width], both[:, width:]
    hidden = (gate / (1.0 + jnp.exp(-gate)) * up).astype(BF)
    for i in range(count):
        outs[i][:, :width] = hidden[i * ROWS : (i + 1) * ROWS]
        outs[i][:, width:] = rows_ref[i * ROWS : (i + 1) * ROWS, model:]


SMALL = pl.CostEstimate(flops=1000, bytes_accessed=1000, transcendentals=0)


def project(weight, blocks, passed, extra=()):
    vmem = pl.BlockSpec(memory_space=pltpu.VMEM)
    there = pl.BlockSpec(memory_space=pl.ANY)
    count = len(blocks)
    out = pl.pallas_call(
        functools.partial(project_kernel, count, passed, len(extra)),
        out_shape=[jax.ShapeDtypeStruct(block.shape, BF) for block in blocks[:passed]]
        + [jax.ShapeDtypeStruct((ROWS, 2 * LANES), BF)] * count,
        in_specs=[vmem] + [there] * (count + len(extra)),
        out_specs=[there] * passed + [vmem] * count,
        input_output_aliases={1 + i: i for i in range(passed)},
        scratch_shapes=[
            pltpu.VMEM((count * ROWS, blocks[0].shape[1]), BF),
            pltpu.SemaphoreType.DMA((count,)),
        ],
        compiler_params=pltpu.CompilerParams(vmem_limit_bytes=24 * 2**20),
        cost_estimate=SMALL,
    )(weight, *blocks, *extra)
    return out[:passed], out[passed:]


def assemble_kernel(plan, low, n_dp, dp_ref, *refs):
    out_ref = refs[-1]
    z = dp_ref[0]
    for s, m, members in plan:
        value = None
        for index, least, most in members:
            part = refs[index][:, low : low + LANES]
            if least > 0 or most < n_dp - 1:
                here = ((z >= least) & (z <= most)).astype(F32)
                part = (part.astype(F32) * here).astype(BF)
            value = part if value is None else value + part
        spot = s * n_dp + lax.rem(z - m + n_dp, n_dp)
        out_ref[pl.ds(pl.multiple_of(spot * ROWS, ROWS), ROWS), :] = value


def assemble(done, low, my_dp):
    plan, flat, known = [], [], {}
    for s, slots in enumerate(done):
        for m, parts in enumerate(slots):
            members = []
            for block, least, most in parts:
                if id(block) not in known:
                    known[id(block)] = len(flat)
                    flat.append(block)
                members.append((known[id(block)], least, most))
            plan.append((s, m, members))
    n_dp = len(done[0])
    vmem = pl.BlockSpec(memory_space=pltpu.VMEM)
    return pl.pallas_call(
        functools.partial(assemble_kernel, plan, low, n_dp),
        out_shape=jax.ShapeDtypeStruct((len(plan) * ROWS, LANES), BF),
        in_specs=[pl.BlockSpec(memory_space=pltpu.SMEM)] + [vmem] * len(flat),
        out_specs=vmem,
        compiler_params=pltpu.CompilerParams(vmem_limit_bytes=8 * 2**20),
        cost_estimate=SMALL,
    )(my_dp.astype(jnp.int32).reshape(1), *flat)


def on_device(
    tokens, experts, replicas, route_weights, slot_tables, partners, slot_rows, gate_w, up_w, down_w
):
    steps, tok, model = tokens.shape
    top = experts.shape[-1]
    n_dp = lax.axis_size("dp")
    columns = lax.axis_size("x") * lax.axis_size("y")
    quad = lax.axis_size("zh") * lax.axis_size("core")
    me = lax.axis_index("zh") * lax.axis_size("core") + lax.axis_index("core")
    column = lax.axis_index("x") * lax.axis_size("y") + lax.axis_index("y")
    my_home = column * quad + me
    my_dp = lax.axis_index("dp")
    mine = steps * tok
    group = quad * tok
    boxes = columns * quad * MOST
    wide = model + LANES
    width = down_w.shape[2]

    right = [[(i, i + 1) for i in range(j, n_dp - 1)] for j in range(n_dp - 1)]
    left = [[(i + 1, i) for i in range(n_dp - 1 - j)] for j in range(n_dp - 1)]

    meta = pack_meta(
        experts.reshape(mine, top),
        replicas.reshape(mine, top),
        route_weights.reshape(mine, top),
        slot_tables[0],
    )
    packed = jnp.concatenate([tokens.reshape(mine, model), meta], axis=1)
    held = lax.all_gather(packed.reshape(steps, tok, wide), ("zh", "core"), axis=1, tiled=True)

    labels = jnp.arange(partners.shape[0], dtype=jnp.int32)
    partner_me = jnp.sum(jnp.where(labels == my_home, partners, 0))
    owners = (my_home, partner_me)
    lanes = jnp.arange(LANES, dtype=jnp.int32)[None, :]
    line = jnp.arange(boxes, dtype=jnp.int32)
    lower = (line[:, None] < line[None, :]).astype(BF)

    def exchange(sets, after=None):
        send = []
        for i, local in enumerate(sets):
            place = places(local[:, model:], me, columns, quad, tok, top)[1]
            if after is not None and i == len(sets) - 1:
                place = place & after
            send.append(
                lax.dot_general(
                    place.astype(BF), local, (((0,), (0,)), ((), ())), preferred_element_type=F32
                )
                .astype(BF)
                .reshape(columns, quad * MOST, wide)
            )
        return lax.all_to_all(
            jnp.concatenate(send, axis=1), ("x", "y"), split_axis=0, concat_axis=0, tiled=True
        )

    def compacted(received, index, local, step, dp, after=None):
        arrived = received[:, index * quad * MOST : (index + 1) * quad * MOST].reshape(boxes, wide)
        valid = arrived[:, model + ONE]
        rank = jnp.dot(valid[None, :], lower, preferred_element_type=F32)
        which = (jnp.arange(n_dp, dtype=jnp.int32)[:, None] == dp) & (
            labels[None, :] == owners[step]
        )
        limit = jnp.sum(jnp.where(which, slot_rows[step], 0)).astype(F32)
        kept = (valid[None, :] > 0) & (rank < limit)
        if after is not None:
            kept = kept & after
        slot_row = jnp.arange(ROWS, dtype=jnp.int32).astype(F32)[:, None]
        chosen = kept & (rank == slot_row)
        pick = chosen.astype(BF)
        compact = jnp.dot(pick, arrived[:, :model], preferred_element_type=F32).astype(BF)
        position = jnp.sum(
            jnp.where(chosen, line.astype(F32)[None, :] + 1.0, 0.0), axis=1, keepdims=True
        )
        side = jnp.pad(local[:, model:], ((0, ROWS - group), (0, 0)))
        side = jnp.where(lanes == POS, position.astype(BF), side)
        return jnp.concatenate([compact, side], axis=1)

    received = exchange([held[step] for step in range(steps)])

    beyond = list(range(STEPS + 1, n_dp))
    half = lax.dynamic_index_in_dim(
        held.reshape(steps, 2, 2, tok, wide), lax.axis_index("core"), 2, keepdims=False
    )
    half = half.reshape(steps * 2 * tok, wide)
    distant = jnp.stack(
        [
            lax.ppermute(
                half,
                "dp",
                [(i, i + k) for i in range(n_dp - k)] + [(i + k, i) for i in range(n_dp - k)],
            )
            for k in beyond
        ]
    ).reshape(len(beyond), steps, 2, tok, wide)
    distant = lax.all_gather(distant, "core", axis=3, tiled=False).reshape(
        len(beyond), steps, group, wide
    )
    both_w = jnp.concatenate([gate_w[0], up_w[0]], axis=1)
    batch = steps * n_dp
    own = [compacted(received, step, held[step], step, my_dp) for step in range(steps)]
    ready = own[-1][0, 0] == own[-1][0, 0]
    received_far = exchange(
        [distant[i, step] for i in range(len(beyond)) for step in range(steps)], ready
    )
    to_right, to_left = list(own), list(own)
    done = [[[] for _ in range(n_dp)] for _ in range(steps)]
    middle = [{} for _ in range(steps)]
    last = n_dp - 1
    hidden = None
    for j in range(1, STEPS + 1):
        for s in range(steps):
            to_right[s] = lax.ppermute(to_right[s], "dp", right[j - 1])
            to_left[s] = lax.ppermute(to_left[s], "dp", left[j - 1])
            blocks = [to_right[s], to_left[s]] + ([own[s]] if j == 1 else [])
            passed = 2 if j < STEPS else 0
            extra = [hidden] if j == EARLY + 1 and s == 0 else []
            extra += [made[0]] if (j, s) != (1, 0) else []
            sent, made = project(both_w, blocks, passed, extra)
            if passed:
                to_right[s], to_left[s] = sent
            if j > EARLY:
                middle[s][j] = made[0][:, :LANES] + made[1][:, :LANES]
            done[s][j].append((made[0], 0, last))
            done[s][n_dp - j].append((made[1], 0, last))
            if j == 1:
                done[s][0].append((made[2], 0, last))
        if j == EARLY:
            ready = made[0][0, 0] == made[0][0, 0]
            blocks = [
                compacted(
                    received_far,
                    i * steps + s,
                    distant[i, s],
                    s,
                    jnp.where(my_dp >= k, my_dp - k, my_dp + k),
                    ready,
                )
                for i, k in enumerate(beyond)
                for s in range(steps)
            ]
            late = project(both_w, blocks, 0)[1]
            for i, k in enumerate(beyond):
                for s in range(steps):
                    done[s][k].append((late[i * steps + s], k, last))
                    done[s][n_dp - k].append((late[i * steps + s], 0, last - k))
            hidden = assemble(
                [
                    [parts if parts else [(done[s][0][0][0], n_dp, n_dp)] for parts in done[s]]
                    for s in range(steps)
                ],
                0,
                my_dp,
            )
    gathered = lax.all_gather(hidden, "dp", axis=0, tiled=False).reshape(
        n_dp, steps, n_dp, ROWS, LANES
    )
    span = range(EARLY + 1, STEPS + 1)
    rest = jnp.stack([jnp.stack([middle[s][k] for k in span]) for s in range(steps)])
    rest = lax.all_to_all(
        jnp.broadcast_to(
            rest.reshape(1, steps * len(span) * ROWS, LANES),
            (n_dp, steps * len(span) * ROWS, LANES),
        ),
        "dp",
        split_axis=0,
        concat_axis=0,
        tiled=True,
    ).reshape(n_dp, steps, len(span), ROWS, LANES)
    for z in range(n_dp):
        for i, k in enumerate(span):
            for d in (z - k, z + k):
                if 0 <= d < n_dp:
                    gathered = lax.dynamic_update_slice(
                        gathered, rest[z : z + 1, :, i : i + 1], (z, 0, d, 0, 0)
                    )
    output = jnp.einsum(
        "zrh,zhf->rf",
        gathered.reshape(n_dp, batch * ROWS, LANES),
        down_w[0].reshape(n_dp, LANES, width),
        preferred_element_type=F32,
    ).astype(BF)

    sides = assemble(done, LANES, my_dp).reshape(batch, ROWS, LANES)

    positions = sides[:, :, POS].astype(jnp.int32) - 1
    unpick = (line[None, :, None] == positions[:, None, :]).astype(BF)
    spread = jnp.einsum(
        "bpr,brf->bpf",
        unpick,
        output.reshape(batch, ROWS, width),
        preferred_element_type=F32,
    ).astype(BF)
    back = lax.all_to_all(
        spread.reshape(batch, columns, quad * MOST, width).transpose(1, 0, 2, 3),
        ("x", "y"),
        split_axis=0,
        concat_axis=0,
        tiled=True,
    )

    token_meta = sides[:, :group].reshape(batch * group, LANES)
    hits, place = places(token_meta, me, columns, quad, tok, top)
    parts = []
    for lane in (HI, MID):
        weight = jnp.zeros((batch * group, boxes), F32)
        for k in range(top):
            weight = jnp.where(
                hits[k], token_meta[:, lane + k : lane + k + 1].astype(F32), weight
            )
        parts.append(jnp.where(place, weight, 0.0).astype(BF).reshape(batch, group, boxes))
    sums = jnp.einsum(
        "btp,bpf->btf",
        jnp.concatenate(parts, axis=1),
        back.transpose(1, 0, 2, 3).reshape(batch, boxes, width),
        preferred_element_type=F32,
    )
    partial = (sums[:, :group] + sums[:, group:]).astype(BF)
    partial = partial.reshape(steps, n_dp, 2, 2, tok, width).transpose(3, 2, 1, 0, 4, 5)
    swapped = lax.all_to_all(partial, "core", split_axis=0, concat_axis=0, tiled=True)
    halves = jnp.sum(swapped.astype(F32), axis=0).astype(BF)
    pieces = lax.all_to_all(
        halves.reshape(2 * n_dp, mine * width // LANES, LANES),
        ("zh", "dp"),
        split_axis=0,
        concat_axis=0,
        tiled=True,
    ).reshape(2, n_dp, mine, width)
    mixed = jnp.sum(pieces.astype(F32), axis=0).astype(BF)
    return mixed.transpose(1, 0, 2).reshape(steps, tok, model)


def solution(mesh):
    names = ("dp", "x", "y", "zh", "core")
    grid = Mesh(mesh.devices.reshape(mesh.shape["dp"], 4, 4, 2, 2), names)
    ep = ("x", "y", "zh", "core")
    rows = P(None, names, None)
    return jax.shard_map(
        on_device,
        mesh=grid,
        in_specs=(
            rows,
            rows,
            rows,
            rows,
            P(),
            P(),
            P(),
            P(ep, None, "dp"),
            P(ep, None, "dp"),
            P(ep, None, "dp"),
        ),
        out_specs=rows,
        check_vma=False,
    )
```

```python
import functools

import jax
import jax.numpy as jnp
from jax import lax
from jax.experimental import pallas as pl
from jax.experimental.pallas import tpu as pltpu
from jax.sharding import Mesh, PartitionSpec as P

BF = jnp.bfloat16
F32 = jnp.float32
LANES = 128
ROWS = 48
MOST = 2
STEPS = 5
NEAR = 4
HOME, HI, MID, ONE, POS = 0, 8, 16, 32, 33


def split_gates(gates):
    high = lax.reduce_precision(gates, 8, 7)
    mid = lax.reduce_precision(gates - high, 8, 7)
    return high.astype(BF), mid.astype(BF)


def pack_meta(experts, replicas, gates, table):
    labels = jnp.arange(table.shape[0], dtype=jnp.int32)
    hot = experts[..., None] == labels
    picked = jnp.where(replicas[..., None] == 0, table[:, 0], table[:, 1])
    home = jnp.sum(jnp.where(hot, picked, 0), axis=-1)
    high, mid = split_gates(gates)
    one = jnp.ones(home.shape, BF)
    meta = jnp.concatenate([home.astype(BF), high, mid, one, one], axis=-1)
    return jnp.pad(meta, ((0, 0), (0, LANES - meta.shape[-1])))


def places(meta, me, columns, quad, tok, top, sets=1):
    n = meta.shape[0]
    box = jnp.arange(columns * sets * quad * MOST, dtype=jnp.int32)[None, :]
    row = jnp.arange(n, dtype=jnp.int32)[:, None]
    target = (box // (sets * quad * MOST) * quad + me).astype(BF)
    same = (row // tok) % (sets * quad) == (box // MOST) % (sets * quad)
    hits = [(meta[:, HOME + k : HOME + k + 1] == target) & same for k in range(top)]
    match = hits[0]
    for hit in hits[1:]:
        match = match | hit
    other = jnp.arange(n, dtype=jnp.int32)[None, :]
    before = ((row // tok == other // tok) & (other < row)).astype(BF)
    earlier = jnp.dot(before, match.astype(BF), preferred_element_type=F32)
    return hits, match & (earlier == (box % MOST).astype(F32))


def project_kernel(count, passed, extra, weight_ref, *refs):
    blocks = refs[:count]
    outs = refs[count + extra + passed : 2 * count + extra + passed]
    rows_ref, sems = refs[-2:]
    width = weight_ref.shape[1] // 2
    model = weight_ref.shape[0]
    copies = [
        pltpu.make_async_copy(
            blocks[i], rows_ref.at[pl.ds(i * ROWS, ROWS)], sems.at[i]
        )
        for i in range(count)
    ]
    for copy in copies:
        copy.start()
    for copy in copies:
        copy.wait()
    both = jnp.dot(rows_ref[:, :model], weight_ref[...], preferred_element_type=F32)
    gate, up = both[:, :width], both[:, width:]
    hidden = (gate / (1.0 + jnp.exp(-gate)) * up).astype(BF)
    for i in range(count):
        outs[i][:, :width] = hidden[i * ROWS : (i + 1) * ROWS]
        outs[i][:, width:] = rows_ref[i * ROWS : (i + 1) * ROWS, model:]


SMALL = pl.CostEstimate(flops=1000, bytes_accessed=1000, transcendentals=0)


def project(weight, blocks, passed, extra=()):
    vmem = pl.BlockSpec(memory_space=pltpu.VMEM)
    there = pl.BlockSpec(memory_space=pl.ANY)
    count = len(blocks)
    out = pl.pallas_call(
        functools.partial(project_kernel, count, passed, len(extra)),
        out_shape=[jax.ShapeDtypeStruct(block.shape, BF) for block in blocks[:passed]]
        + [jax.ShapeDtypeStruct((ROWS, 2 * LANES), BF)] * count,
        in_specs=[vmem] + [there] * (count + len(extra)),
        out_specs=[there] * passed + [vmem] * count,
        input_output_aliases={1 + i: i for i in range(passed)},
        scratch_shapes=[
            pltpu.VMEM((count * ROWS, blocks[0].shape[1]), BF),
            pltpu.SemaphoreType.DMA((count,)),
        ],
        compiler_params=pltpu.CompilerParams(vmem_limit_bytes=24 * 2**20),
        cost_estimate=SMALL,
    )(weight, *blocks, *extra)
    return out[:passed], out[passed:]


def assemble_kernel(plan, low, n_dp, dp_ref, *refs):
    out_ref = refs[-1]
    z = dp_ref[0]
    for s, m, members in plan:
        value = None
        for index, least, most in members:
            part = refs[index][:, low : low + LANES]
            if least > 0 or most < n_dp - 1:
                here = ((z >= least) & (z <= most)).astype(F32)
                part = (part.astype(F32) * here).astype(BF)
            value = part if value is None else value + part
        spot = s * n_dp + lax.rem(z - m + n_dp, n_dp)
        out_ref[pl.ds(pl.multiple_of(spot * ROWS, ROWS), ROWS), :] = value


def assemble(done, low, my_dp):
    plan, flat, known = [], [], {}
    for s, slots in enumerate(done):
        for m, parts in enumerate(slots):
            members = []
            for block, least, most in parts:
                if id(block) not in known:
                    known[id(block)] = len(flat)
                    flat.append(block)
                members.append((known[id(block)], least, most))
            plan.append((s, m, members))
    n_dp = len(done[0])
    vmem = pl.BlockSpec(memory_space=pltpu.VMEM)
    return pl.pallas_call(
        functools.partial(assemble_kernel, plan, low, n_dp),
        out_shape=jax.ShapeDtypeStruct((len(plan) * ROWS, LANES), BF),
        in_specs=[pl.BlockSpec(memory_space=pltpu.SMEM)] + [vmem] * len(flat),
        out_specs=vmem,
        compiler_params=pltpu.CompilerParams(vmem_limit_bytes=8 * 2**20),
        cost_estimate=SMALL,
    )(my_dp.astype(jnp.int32).reshape(1), *flat)


def down_kernel(places_of, n_dp, dp_ref, down_ref, *refs):
    out_ref = refs[-1]
    z = dp_ref[0]
    total = None
    for i in range(0, len(places_of), 2):
        pair = range(i, min(i + 2, len(places_of)))
        weights = [
            down_ref[pl.ds(pl.multiple_of(places_of[p](z) * LANES, LANES), LANES), :] for p in pair
        ]
        part = jnp.dot(
            jnp.concatenate([refs[p][...] for p in pair], axis=1),
            jnp.concatenate(weights, axis=0),
            preferred_element_type=F32,
        )
        total = part if total is None else total + part
    out_ref[...] = total.astype(BF)


def project_down(shards, places_of, down, n_dp, my_dp):
    vmem = pl.BlockSpec(memory_space=pltpu.VMEM)
    return pl.pallas_call(
        functools.partial(down_kernel, places_of, n_dp),
        out_shape=jax.ShapeDtypeStruct((shards[0].shape[0], down.shape[1]), BF),
        in_specs=[pl.BlockSpec(memory_space=pltpu.SMEM), vmem] + [vmem] * len(shards),
        out_specs=vmem,
        compiler_params=pltpu.CompilerParams(vmem_limit_bytes=32 * 2**20),
        cost_estimate=SMALL,
    )(my_dp.astype(jnp.int32).reshape(1), down, *shards)


def on_device(
    tokens, experts, replicas, route_weights, slot_tables, partners, slot_rows, gate_w, up_w, down_w
):
    steps, tok, model = tokens.shape
    top = experts.shape[-1]
    n_dp = lax.axis_size("dp")
    columns = lax.axis_size("x") * lax.axis_size("y")
    quad = lax.axis_size("zh") * lax.axis_size("core")
    me = lax.axis_index("zh") * lax.axis_size("core") + lax.axis_index("core")
    column = lax.axis_index("x") * lax.axis_size("y") + lax.axis_index("y")
    my_home = column * quad + me
    my_dp = lax.axis_index("dp")
    mine = steps * tok
    group = quad * tok
    boxes = columns * quad * MOST
    wide = model + LANES
    width = down_w.shape[2]

    right = [[(i, i + 1) for i in range(j, n_dp - 1)] for j in range(n_dp - 1)]
    left = [[(i + 1, i) for i in range(n_dp - 1 - j)] for j in range(n_dp - 1)]

    meta = pack_meta(
        experts.reshape(mine, top),
        replicas.reshape(mine, top),
        route_weights.reshape(mine, top),
        slot_tables[0],
    )
    packed = jnp.concatenate([tokens.reshape(mine, model), meta], axis=1)
    held = lax.all_gather(packed.reshape(steps, tok, wide), ("zh", "core"), axis=1, tiled=True)

    labels = jnp.arange(partners.shape[0], dtype=jnp.int32)
    partner_me = jnp.sum(jnp.where(labels == my_home, partners, 0))
    owners = (my_home, partner_me)
    lanes = jnp.arange(LANES, dtype=jnp.int32)[None, :]
    line = jnp.arange(boxes, dtype=jnp.int32)
    lower = (line[:, None] < line[None, :]).astype(BF)

    def exchange(local, sets, after=None):
        place = places(local[:, model:], me, columns, quad, tok, top, sets)[1]
        if after is not None:
            place = place & after
        send = lax.dot_general(
            place.astype(BF), local, (((0,), (0,)), ((), ())), preferred_element_type=F32
        ).astype(BF)
        return lax.all_to_all(
            send.reshape(columns, sets * quad * MOST, wide),
            ("x", "y"),
            split_axis=0,
            concat_axis=0,
            tiled=True,
        )

    def compacted(received, index, local, step, dp, after=None):
        arrived = received[:, index * quad * MOST : (index + 1) * quad * MOST].reshape(boxes, wide)
        valid = arrived[:, model + ONE]
        rank = jnp.dot(valid[None, :], lower, preferred_element_type=F32)
        which = (jnp.arange(n_dp, dtype=jnp.int32)[:, None] == dp) & (
            labels[None, :] == owners[step]
        )
        limit = jnp.sum(jnp.where(which, slot_rows[step], 0)).astype(F32)
        kept = (valid[None, :] > 0) & (rank < limit)
        if after is not None:
            kept = kept & after
        slot_row = jnp.arange(ROWS, dtype=jnp.int32).astype(F32)[:, None]
        chosen = kept & (rank == slot_row)
        pick = chosen.astype(BF)
        compact = jnp.dot(pick, arrived[:, :model], preferred_element_type=F32).astype(BF)
        position = jnp.sum(
            jnp.where(chosen, line.astype(F32)[None, :] + 1.0, 0.0), axis=1, keepdims=True
        )
        side = jnp.pad(local[:, model:], ((0, ROWS - group), (0, 0)))
        side = jnp.where(lanes == POS, position.astype(BF), side)
        return jnp.concatenate([compact, side], axis=1)

    held_rows = held.reshape(steps * group, wide)
    received = exchange(held_rows, steps)

    both_w = jnp.concatenate([gate_w[0], up_w[0]], axis=1)
    batch = steps * n_dp
    own = [compacted(received, step, held[step], step, my_dp) for step in range(steps)]
    beyond = list(range(STEPS + 1, n_dp))
    apart = {
        k: [(i, i + k) for i in range(n_dp - k)] + [(i + k, i) for i in range(n_dp - k)]
        for k in range(NEAR + 1, n_dp)
    }
    leaving = jnp.where(own[-1][0, 0] == own[-1][0, 0], held_rows, jnp.zeros_like(held_rows))
    distant = jnp.concatenate([lax.ppermute(leaving, "dp", apart[k]) for k in beyond], axis=0)

    to_right, to_left = list(own), list(own)
    done = [[[] for _ in range(n_dp)] for _ in range(steps)]
    last = n_dp - 1
    for j in range(1, STEPS + 1):
        for s in range(steps):
            to_right[s] = lax.ppermute(to_right[s], "dp", right[j - 1])
            to_left[s] = lax.ppermute(to_left[s], "dp", left[j - 1])
            blocks = [to_right[s], to_left[s]] + ([own[s]] if j == 1 else [])
            passed = 2 if j < STEPS else 0
            extra = [late[0]] if j == STEPS and s == 0 else []
            extra += [made[0]] if (j, s) != (1, 0) else []
            sent, made = project(both_w, blocks, passed, extra)
            if passed:
                to_right[s], to_left[s] = sent
            done[s][j].append((made[0], 0, last))
            done[s][n_dp - j].append((made[1], 0, last))
            if j == 1:
                done[s][0].append((made[2], 0, last))
            if (j, s) == (1, steps - 1):
                received_far = exchange(
                    distant, len(beyond) * steps, made[0][0, 0] == made[0][0, 0]
                )
        if j == STEPS - 1:
            ready = made[0][0, 0] == made[0][0, 0]
            late = project(
                both_w,
                [
                    compacted(
                        received_far,
                        i * steps + s,
                        distant[(i * steps + s) * group : (i * steps + s + 1) * group],
                        s,
                        jnp.where(my_dp >= k, my_dp - k, my_dp + k),
                        ready,
                    )
                    for i, k in enumerate(beyond)
                    for s in range(steps)
                ],
                0,
            )[1]
            for i, k in enumerate(beyond):
                for s in range(steps):
                    done[s][k].append((late[i * steps + s], k, last))
                    done[s][n_dp - k].append((late[i * steps + s], 0, last - k))
    hidden = assemble(done, 0, my_dp)
    shards, places_of = [hidden], [lambda z: z]
    going_right, going_left = hidden, hidden
    for k in range(NEAR + 1, n_dp):
        shards.append(lax.ppermute(hidden, "dp", apart[k]))
        places_of.append(lambda z, k=k: lax.rem(jnp.where(z >= k, z - k, z + k), n_dp))
    for j in range(1, NEAR + 1):
        going_right = lax.ppermute(going_right, "dp", right[j - 1])
        going_left = lax.ppermute(going_left, "dp", left[j - 1])
        shards += [going_right, going_left]
        places_of.append(lambda z, j=j: lax.rem(z - j + n_dp, n_dp))
        places_of.append(lambda z, j=j: lax.rem(z + j, n_dp))
    output = project_down(shards, places_of, down_w[0], n_dp, my_dp)

    sides = assemble(done, LANES, my_dp).reshape(batch, ROWS, LANES)

    positions = sides[:, :, POS].astype(jnp.int32) - 1
    unpick = (line[None, :, None] == positions[:, None, :]).astype(BF)
    spread = jnp.einsum(
        "bpr,brf->bpf",
        unpick,
        output.reshape(batch, ROWS, width),
        preferred_element_type=F32,
    ).astype(BF)
    back = lax.all_to_all(
        spread.reshape(batch, columns, quad * MOST, width).transpose(1, 0, 2, 3),
        ("x", "y"),
        split_axis=0,
        concat_axis=0,
        tiled=True,
    )

    token_meta = sides[:, :group].reshape(batch * group, LANES)
    hits, place = places(token_meta, me, columns, quad, tok, top)
    parts = []
    for lane in (HI, MID):
        weight = jnp.zeros((batch * group, boxes), F32)
        for k in range(top):
            weight = jnp.where(
                hits[k], token_meta[:, lane + k : lane + k + 1].astype(F32), weight
            )
        parts.append(jnp.where(place, weight, 0.0).astype(BF).reshape(batch, group, boxes))
    sums = jnp.einsum(
        "btp,bpf->btf",
        jnp.concatenate(parts, axis=1),
        back.transpose(1, 0, 2, 3).reshape(batch, boxes, width),
        preferred_element_type=F32,
    )
    partial = (sums[:, :group] + sums[:, group:]).astype(BF)
    partial = partial.reshape(steps, n_dp, 2, 2, tok, width).transpose(3, 2, 1, 0, 4, 5)
    swapped = lax.all_to_all(partial, "core", split_axis=0, concat_axis=0, tiled=True)
    halves = jnp.sum(swapped.astype(F32), axis=0).astype(BF)
    pieces = lax.all_to_all(
        halves.reshape(2 * n_dp, mine * width // LANES, LANES),
        ("zh", "dp"),
        split_axis=0,
        concat_axis=0,
        tiled=True,
    ).reshape(2, n_dp, mine, width)
    mixed = jnp.sum(pieces.astype(F32), axis=0).astype(BF)
    return mixed.transpose(1, 0, 2).reshape(steps, tok, model)


def solution(mesh):
    names = ("dp", "x", "y", "zh", "core")
    grid = Mesh(mesh.devices.reshape(mesh.shape["dp"], 4, 4, 2, 2), names)
    ep = ("x", "y", "zh", "core")
    rows = P(None, names, None)
    return jax.shard_map(
        on_device,
        mesh=grid,
        in_specs=(
            rows,
            rows,
            rows,
            rows,
            P(),
            P(),
            P(),
            P(ep, None, "dp"),
            P(ep, None, "dp"),
            P(ep, None, "dp"),
        ),
        out_specs=rows,
        check_vma=False,
    )
```

```python
import functools

import jax
import jax.numpy as jnp
from jax import lax
from jax.experimental import pallas as pl
from jax.experimental.pallas import tpu as pltpu
from jax.sharding import Mesh, PartitionSpec as P

BF = jnp.bfloat16
F32 = jnp.float32
LANES = 128
ROWS = 48
MOST = 2
STEPS = 5
NEAR = 5
HOME, HI, MID, ONE, POS = 0, 8, 16, 32, 33


def split_gates(gates):
    high = lax.reduce_precision(gates, 8, 7)
    mid = lax.reduce_precision(gates - high, 8, 7)
    return high.astype(BF), mid.astype(BF)


def pack_meta(experts, replicas, gates, table):
    labels = jnp.arange(table.shape[0], dtype=jnp.int32)
    hot = experts[..., None] == labels
    picked = jnp.where(replicas[..., None] == 0, table[:, 0], table[:, 1])
    home = jnp.sum(jnp.where(hot, picked, 0), axis=-1)
    high, mid = split_gates(gates)
    one = jnp.ones(home.shape, BF)
    meta = jnp.concatenate([home.astype(BF), high, mid, one, one], axis=-1)
    return jnp.pad(meta, ((0, 0), (0, LANES - meta.shape[-1])))


def places(meta, me, columns, quad, tok, top, sets=1):
    n = meta.shape[0]
    box = jnp.arange(columns * sets * quad * MOST, dtype=jnp.int32)[None, :]
    row = jnp.arange(n, dtype=jnp.int32)[:, None]
    target = (box // (sets * quad * MOST) * quad + me).astype(BF)
    same = (row // tok) % (sets * quad) == (box // MOST) % (sets * quad)
    hits = [(meta[:, HOME + k : HOME + k + 1] == target) & same for k in range(top)]
    match = hits[0]
    for hit in hits[1:]:
        match = match | hit
    other = jnp.arange(n, dtype=jnp.int32)[None, :]
    before = ((row // tok == other // tok) & (other < row)).astype(BF)
    earlier = jnp.dot(before, match.astype(BF), preferred_element_type=F32)
    return hits, match & (earlier == (box % MOST).astype(F32))


def project_kernel(count, passed, extra, weight_ref, *refs):
    blocks = refs[:count]
    outs = refs[count + extra + passed : 2 * count + extra + passed]
    rows_ref, sems = refs[-2:]
    width = weight_ref.shape[1] // 2
    model = weight_ref.shape[0]
    copies = [
        pltpu.make_async_copy(
            blocks[i], rows_ref.at[pl.ds(i * ROWS, ROWS)], sems.at[i]
        )
        for i in range(count)
    ]
    for copy in copies:
        copy.start()
    for copy in copies:
        copy.wait()
    both = jnp.dot(rows_ref[:, :model], weight_ref[...], preferred_element_type=F32)
    gate, up = both[:, :width], both[:, width:]
    hidden = (gate / (1.0 + jnp.exp(-gate)) * up).astype(BF)
    for i in range(count):
        outs[i][:, :width] = hidden[i * ROWS : (i + 1) * ROWS]
        outs[i][:, width:] = rows_ref[i * ROWS : (i + 1) * ROWS, model:]


SMALL = pl.CostEstimate(flops=1000, bytes_accessed=1000, transcendentals=0)


def project(weight, blocks, passed, extra=()):
    vmem = pl.BlockSpec(memory_space=pltpu.VMEM)
    there = pl.BlockSpec(memory_space=pl.ANY)
    count = len(blocks)
    out = pl.pallas_call(
        functools.partial(project_kernel, count, passed, len(extra)),
        out_shape=[jax.ShapeDtypeStruct(block.shape, BF) for block in blocks[:passed]]
        + [jax.ShapeDtypeStruct((ROWS, 2 * LANES), BF)] * count,
        in_specs=[vmem] + [there] * (count + len(extra)),
        out_specs=[there] * passed + [vmem] * count,
        input_output_aliases={1 + i: i for i in range(passed)},
        scratch_shapes=[
            pltpu.VMEM((count * ROWS, blocks[0].shape[1]), BF),
            pltpu.SemaphoreType.DMA((count,)),
        ],
        compiler_params=pltpu.CompilerParams(vmem_limit_bytes=24 * 2**20),
        cost_estimate=SMALL,
    )(weight, *blocks, *extra)
    return out[:passed], out[passed:]


def assemble_kernel(plan, low, n_dp, dp_ref, *refs):
    out_ref = refs[-1]
    z = dp_ref[0]
    for s, m, members in plan:
        value = None
        for index, least, most in members:
            part = refs[index][:, low : low + LANES]
            if least > 0 or most < n_dp - 1:
                here = ((z >= least) & (z <= most)).astype(F32)
                part = (part.astype(F32) * here).astype(BF)
            value = part if value is None else value + part
        spot = s * n_dp + lax.rem(z - m + n_dp, n_dp)
        out_ref[pl.ds(pl.multiple_of(spot * ROWS, ROWS), ROWS), :] = value


def assemble(done, low, my_dp):
    plan, flat, known = [], [], {}
    for s, slots in enumerate(done):
        for m, parts in enumerate(slots):
            members = []
            for block, least, most in parts:
                if id(block) not in known:
                    known[id(block)] = len(flat)
                    flat.append(block)
                members.append((known[id(block)], least, most))
            plan.append((s, m, members))
    n_dp = len(done[0])
    vmem = pl.BlockSpec(memory_space=pltpu.VMEM)
    return pl.pallas_call(
        functools.partial(assemble_kernel, plan, low, n_dp),
        out_shape=jax.ShapeDtypeStruct((len(plan) * ROWS, LANES), BF),
        in_specs=[pl.BlockSpec(memory_space=pltpu.SMEM)] + [vmem] * len(flat),
        out_specs=vmem,
        compiler_params=pltpu.CompilerParams(vmem_limit_bytes=8 * 2**20),
        cost_estimate=SMALL,
    )(my_dp.astype(jnp.int32).reshape(1), *flat)


def down_kernel(places_of, n_dp, dp_ref, down_ref, *refs):
    out_ref = refs[-1]
    z = dp_ref[0]
    total = None
    for i in range(0, len(places_of), 2):
        pair = range(i, min(i + 2, len(places_of)))
        weights = [
            down_ref[pl.ds(pl.multiple_of(places_of[p](z) * LANES, LANES), LANES), :] for p in pair
        ]
        part = jnp.dot(
            jnp.concatenate([refs[p][...] for p in pair], axis=1),
            jnp.concatenate(weights, axis=0),
            preferred_element_type=F32,
        )
        total = part if total is None else total + part
    out_ref[...] = total.astype(BF)


def project_down(shards, places_of, down, n_dp, my_dp):
    vmem = pl.BlockSpec(memory_space=pltpu.VMEM)
    return pl.pallas_call(
        functools.partial(down_kernel, places_of, n_dp),
        out_shape=jax.ShapeDtypeStruct((shards[0].shape[0], down.shape[1]), BF),
        in_specs=[pl.BlockSpec(memory_space=pltpu.SMEM), vmem] + [vmem] * len(shards),
        out_specs=vmem,
        compiler_params=pltpu.CompilerParams(vmem_limit_bytes=32 * 2**20),
        cost_estimate=SMALL,
    )(my_dp.astype(jnp.int32).reshape(1), down, *shards)


def on_device(
    tokens, experts, replicas, route_weights, slot_tables, partners, slot_rows, gate_w, up_w, down_w
):
    steps, tok, model = tokens.shape
    top = experts.shape[-1]
    n_dp = lax.axis_size("dp")
    columns = lax.axis_size("x") * lax.axis_size("y")
    quad = lax.axis_size("zh") * lax.axis_size("core")
    me = lax.axis_index("zh") * lax.axis_size("core") + lax.axis_index("core")
    column = lax.axis_index("x") * lax.axis_size("y") + lax.axis_index("y")
    my_home = column * quad + me
    my_dp = lax.axis_index("dp")
    mine = steps * tok
    group = quad * tok
    boxes = columns * quad * MOST
    wide = model + LANES
    width = down_w.shape[2]

    right = [[(i, i + 1) for i in range(j, n_dp - 1)] for j in range(n_dp - 1)]
    left = [[(i + 1, i) for i in range(n_dp - 1 - j)] for j in range(n_dp - 1)]

    meta = pack_meta(
        experts.reshape(mine, top),
        replicas.reshape(mine, top),
        route_weights.reshape(mine, top),
        slot_tables[0],
    )
    packed = jnp.concatenate([tokens.reshape(mine, model), meta], axis=1)
    held = lax.all_gather(packed.reshape(steps, tok, wide), ("zh", "core"), axis=1, tiled=True)

    labels = jnp.arange(partners.shape[0], dtype=jnp.int32)
    partner_me = jnp.sum(jnp.where(labels == my_home, partners, 0))
    owners = (my_home, partner_me)
    lanes = jnp.arange(LANES, dtype=jnp.int32)[None, :]
    line = jnp.arange(boxes, dtype=jnp.int32)
    lower = (line[:, None] < line[None, :]).astype(BF)

    def exchange(local, sets, after=None):
        place = places(local[:, model:], me, columns, quad, tok, top, sets)[1]
        if after is not None:
            place = place & after
        send = lax.dot_general(
            place.astype(BF), local, (((0,), (0,)), ((), ())), preferred_element_type=F32
        ).astype(BF)
        return lax.all_to_all(
            send.reshape(columns, sets * quad * MOST, wide),
            ("x", "y"),
            split_axis=0,
            concat_axis=0,
            tiled=True,
        )

    def compacted(received, index, local, step, dp, after=None):
        arrived = received[:, index * quad * MOST : (index + 1) * quad * MOST].reshape(boxes, wide)
        valid = arrived[:, model + ONE]
        rank = jnp.dot(valid[None, :], lower, preferred_element_type=F32)
        which = (jnp.arange(n_dp, dtype=jnp.int32)[:, None] == dp) & (
            labels[None, :] == owners[step]
        )
        limit = jnp.sum(jnp.where(which, slot_rows[step], 0)).astype(F32)
        kept = (valid[None, :] > 0) & (rank < limit)
        if after is not None:
            kept = kept & after
        slot_row = jnp.arange(ROWS, dtype=jnp.int32).astype(F32)[:, None]
        chosen = kept & (rank == slot_row)
        pick = chosen.astype(BF)
        compact = jnp.dot(pick, arrived[:, :model], preferred_element_type=F32).astype(BF)
        position = jnp.sum(
            jnp.where(chosen, line.astype(F32)[None, :] + 1.0, 0.0), axis=1, keepdims=True
        )
        side = jnp.pad(local[:, model:], ((0, ROWS - group), (0, 0)))
        side = jnp.where(lanes == POS, position.astype(BF), side)
        return jnp.concatenate([compact, side], axis=1)

    held_rows = held.reshape(steps * group, wide)
    received = exchange(held_rows, steps)

    both_w = jnp.concatenate([gate_w[0], up_w[0]], axis=1)
    batch = steps * n_dp
    own = [compacted(received, step, held[step], step, my_dp) for step in range(steps)]
    beyond = list(range(STEPS + 1, n_dp))
    apart = {
        k: [(i, i + k) for i in range(n_dp - k)] + [(i + k, i) for i in range(n_dp - k)]
        for k in range(NEAR + 1, n_dp)
    }
    leaving = jnp.where(own[-1][0, 0] == own[-1][0, 0], held_rows, jnp.zeros_like(held_rows))
    distant = jnp.concatenate([lax.ppermute(leaving, "dp", apart[k]) for k in beyond], axis=0)

    to_right, to_left = list(own), list(own)
    done = [[[] for _ in range(n_dp)] for _ in range(steps)]
    last = n_dp - 1
    for j in range(1, STEPS + 1):
        for s in range(steps):
            to_right[s] = lax.ppermute(to_right[s], "dp", right[j - 1])
            to_left[s] = lax.ppermute(to_left[s], "dp", left[j - 1])
            blocks = [to_right[s], to_left[s]] + ([own[s]] if j == 1 else [])
            passed = 2 if j < STEPS else 0
            extra = [made[0]] if (j, s) != (1, 0) else []
            sent, made = project(both_w, blocks, passed, extra)
            if passed:
                to_right[s], to_left[s] = sent
            done[s][j].append((made[0], 0, last))
            done[s][n_dp - j].append((made[1], 0, last))
            if j == 1:
                done[s][0].append((made[2], 0, last))
            if (j, s) == (2, steps - 1):
                received_far = exchange(
                    distant, len(beyond) * steps, made[0][0, 0] == made[0][0, 0]
                )
        if j == STEPS:
            ready = made[0][0, 0] == made[0][0, 0]
            late = project(
                both_w,
                [
                    compacted(
                        received_far,
                        i * steps + s,
                        distant[(i * steps + s) * group : (i * steps + s + 1) * group],
                        s,
                        jnp.where(my_dp >= k, my_dp - k, my_dp + k),
                        ready,
                    )
                    for i, k in enumerate(beyond)
                    for s in range(steps)
                ],
                0,
            )[1]
            for i, k in enumerate(beyond):
                for s in range(steps):
                    done[s][k].append((late[i * steps + s], k, last))
                    done[s][n_dp - k].append((late[i * steps + s], 0, last - k))
    hidden = assemble(done, 0, my_dp)
    shards, places_of = [hidden], [lambda z: z]
    going_right, going_left = hidden, hidden
    for k in range(NEAR + 1, n_dp):
        shards.append(lax.ppermute(hidden, "dp", apart[k]))
        places_of.append(lambda z, k=k: lax.rem(jnp.where(z >= k, z - k, z + k), n_dp))
    for j in range(1, NEAR + 1):
        going_right = lax.ppermute(going_right, "dp", right[j - 1])
        going_left = lax.ppermute(going_left, "dp", left[j - 1])
        shards += [going_right, going_left]
        places_of.append(lambda z, j=j: lax.rem(z - j + n_dp, n_dp))
        places_of.append(lambda z, j=j: lax.rem(z + j, n_dp))
    output = project_down(shards, places_of, down_w[0], n_dp, my_dp)

    sides = assemble(done, LANES, my_dp).reshape(batch, ROWS, LANES)

    positions = sides[:, :, POS].astype(jnp.int32) - 1
    unpick = (line[None, :, None] == positions[:, None, :]).astype(BF)
    spread = jnp.einsum(
        "bpr,brf->bpf",
        unpick,
        output.reshape(batch, ROWS, width),
        preferred_element_type=F32,
    ).astype(BF)
    back = lax.all_to_all(
        spread.reshape(batch, columns, quad * MOST, width).transpose(1, 0, 2, 3),
        ("x", "y"),
        split_axis=0,
        concat_axis=0,
        tiled=True,
    )

    token_meta = sides[:, :group].reshape(batch * group, LANES)
    hits, place = places(token_meta, me, columns, quad, tok, top)
    parts = []
    for lane in (HI, MID):
        weight = jnp.zeros((batch * group, boxes), F32)
        for k in range(top):
            weight = jnp.where(
                hits[k], token_meta[:, lane + k : lane + k + 1].astype(F32), weight
            )
        parts.append(jnp.where(place, weight, 0.0).astype(BF).reshape(batch, group, boxes))
    sums = jnp.einsum(
        "btp,bpf->btf",
        jnp.concatenate(parts, axis=1),
        back.transpose(1, 0, 2, 3).reshape(batch, boxes, width),
        preferred_element_type=F32,
    )
    partial = (sums[:, :group] + sums[:, group:]).astype(BF)
    partial = partial.reshape(steps, n_dp, 2, 2, tok, width).transpose(3, 2, 1, 0, 4, 5)
    swapped = lax.all_to_all(partial, "core", split_axis=0, concat_axis=0, tiled=True)
    halves = jnp.sum(swapped.astype(F32), axis=0).astype(BF)
    pieces = lax.all_to_all(
        halves.reshape(2 * n_dp, mine * width // LANES, LANES),
        ("zh", "dp"),
        split_axis=0,
        concat_axis=0,
        tiled=True,
    ).reshape(2, n_dp, mine, width)
    mixed = jnp.sum(pieces.astype(F32), axis=0).astype(BF)
    return mixed.transpose(1, 0, 2).reshape(steps, tok, model)


def solution(mesh):
    names = ("dp", "x", "y", "zh", "core")
    grid = Mesh(mesh.devices.reshape(mesh.shape["dp"], 4, 4, 2, 2), names)
    ep = ("x", "y", "zh", "core")
    rows = P(None, names, None)
    return jax.shard_map(
        on_device,
        mesh=grid,
        in_specs=(
            rows,
            rows,
            rows,
            rows,
            P(),
            P(),
            P(),
            P(ep, None, "dp"),
            P(ep, None, "dp"),
            P(ep, None, "dp"),
        ),
        out_specs=rows,
        check_vma=False,
    )
```

```python
import functools

import jax
import jax.numpy as jnp
from jax import lax
from jax.experimental import pallas as pl
from jax.experimental.pallas import tpu as pltpu
from jax.sharding import Mesh, PartitionSpec as P

BF = jnp.bfloat16
F32 = jnp.float32
LANES = 128
ROWS = 48
MOST = 2
HOME, HI, MID, ONE, POS = 0, 8, 16, 32, 33


def split_gates(gates):
    high = lax.reduce_precision(gates, 8, 7)
    mid = lax.reduce_precision(gates - high, 8, 7)
    return high.astype(BF), mid.astype(BF)


def pack_meta(experts, replicas, gates, table):
    labels = jnp.arange(table.shape[0], dtype=jnp.int32)
    hot = experts[..., None] == labels
    picked = jnp.where(replicas[..., None] == 0, table[:, 0], table[:, 1])
    home = jnp.sum(jnp.where(hot, picked, 0), axis=-1)
    high, mid = split_gates(gates)
    one = jnp.ones(home.shape, BF)
    meta = jnp.concatenate([home.astype(BF), high, mid, one, one], axis=-1)
    return jnp.pad(meta, ((0, 0), (0, LANES - meta.shape[-1])))


def places(meta, me, columns, quad, tok, top, sets=1):
    n = meta.shape[0]
    box = jnp.arange(columns * sets * quad * MOST, dtype=jnp.int32)[None, :]
    row = jnp.arange(n, dtype=jnp.int32)[:, None]
    target = (box // (sets * quad * MOST) * quad + me).astype(BF)
    same = (row // tok) % (sets * quad) == (box // MOST) % (sets * quad)
    hits = [(meta[:, HOME + k : HOME + k + 1] == target) & same for k in range(top)]
    match = hits[0]
    for hit in hits[1:]:
        match = match | hit
    other = jnp.arange(n, dtype=jnp.int32)[None, :]
    before = ((row // tok == other // tok) & (other < row)).astype(BF)
    earlier = jnp.dot(before, match.astype(BF), preferred_element_type=F32)
    return hits, match & (earlier == (box % MOST).astype(F32))


def project_kernel(count, passed, extra, weight_ref, *refs):
    blocks = refs[:count]
    outs = refs[count + extra + passed : 2 * count + extra + passed]
    rows_ref, sems = refs[-2:]
    width = weight_ref.shape[1] // 2
    model = weight_ref.shape[0]
    copies = [
        pltpu.make_async_copy(
            blocks[i], rows_ref.at[pl.ds(i * ROWS, ROWS)], sems.at[i]
        )
        for i in range(count)
    ]
    for copy in copies:
        copy.start()
    for copy in copies:
        copy.wait()
    both = jnp.dot(rows_ref[:, :model], weight_ref[...], preferred_element_type=F32)
    gate, up = both[:, :width], both[:, width:]
    hidden = (gate / (1.0 + jnp.exp(-gate)) * up).astype(BF)
    for i in range(count):
        outs[i][:, :width] = hidden[i * ROWS : (i + 1) * ROWS]
        outs[i][:, width:] = rows_ref[i * ROWS : (i + 1) * ROWS, model:]


SMALL = pl.CostEstimate(flops=1000, bytes_accessed=1000, transcendentals=0)


def project(weight, blocks, passed, extra=()):
    vmem = pl.BlockSpec(memory_space=pltpu.VMEM)
    there = pl.BlockSpec(memory_space=pl.ANY)
    count = len(blocks)
    out = pl.pallas_call(
        functools.partial(project_kernel, count, passed, len(extra)),
        out_shape=[jax.ShapeDtypeStruct(block.shape, BF) for block in blocks[:passed]]
        + [jax.ShapeDtypeStruct((ROWS, 2 * LANES), BF)] * count,
        in_specs=[vmem] + [there] * (count + len(extra)),
        out_specs=[there] * passed + [vmem] * count,
        input_output_aliases={1 + i: i for i in range(passed)},
        scratch_shapes=[
            pltpu.VMEM((count * ROWS, blocks[0].shape[1]), BF),
            pltpu.SemaphoreType.DMA((count,)),
        ],
        compiler_params=pltpu.CompilerParams(vmem_limit_bytes=24 * 2**20),
        cost_estimate=SMALL,
    )(weight, *blocks, *extra)
    return out[:passed], out[passed:]


def assemble_kernel(plan, low, n_dp, dp_ref, *refs):
    out_ref = refs[-1]
    z = dp_ref[0]
    for s, m, members in plan:
        value = None
        for index, least, most in members:
            part = refs[index][:, low : low + LANES]
            if least > 0 or most < n_dp - 1:
                here = ((z >= least) & (z <= most)).astype(F32)
                part = (part.astype(F32) * here).astype(BF)
            value = part if value is None else value + part
        spot = s * n_dp + lax.rem(z - m + n_dp, n_dp)
        out_ref[pl.ds(pl.multiple_of(spot * ROWS, ROWS), ROWS), :] = value


def assemble(done, low, my_dp):
    plan, flat, known = [], [], {}
    for s, slots in enumerate(done):
        for m, parts in enumerate(slots):
            members = []
            for block, least, most in parts:
                if id(block) not in known:
                    known[id(block)] = len(flat)
                    flat.append(block)
                members.append((known[id(block)], least, most))
            plan.append((s, m, members))
    n_dp = len(done[0])
    vmem = pl.BlockSpec(memory_space=pltpu.VMEM)
    return pl.pallas_call(
        functools.partial(assemble_kernel, plan, low, n_dp),
        out_shape=jax.ShapeDtypeStruct((len(plan) * ROWS, LANES), BF),
        in_specs=[pl.BlockSpec(memory_space=pltpu.SMEM)] + [vmem] * len(flat),
        out_specs=vmem,
        compiler_params=pltpu.CompilerParams(vmem_limit_bytes=8 * 2**20),
        cost_estimate=SMALL,
    )(my_dp.astype(jnp.int32).reshape(1), *flat)


def down_kernel(places_of, n_dp, dp_ref, down_ref, *refs):
    out_ref = refs[-1]
    z = dp_ref[0]
    total = None
    for i in range(0, len(places_of), 2):
        pair = range(i, min(i + 2, len(places_of)))
        weights = [
            down_ref[pl.ds(pl.multiple_of(places_of[p](z) * LANES, LANES), LANES), :] for p in pair
        ]
        part = jnp.dot(
            jnp.concatenate([refs[p][...] for p in pair], axis=1),
            jnp.concatenate(weights, axis=0),
            preferred_element_type=F32,
        )
        total = part if total is None else total + part
    out_ref[...] = total.astype(BF)


def project_down(shards, places_of, down, n_dp, my_dp):
    vmem = pl.BlockSpec(memory_space=pltpu.VMEM)
    return pl.pallas_call(
        functools.partial(down_kernel, places_of, n_dp),
        out_shape=jax.ShapeDtypeStruct((shards[0].shape[0], down.shape[1]), BF),
        in_specs=[pl.BlockSpec(memory_space=pltpu.SMEM), vmem] + [vmem] * len(shards),
        out_specs=vmem,
        compiler_params=pltpu.CompilerParams(vmem_limit_bytes=32 * 2**20),
        cost_estimate=SMALL,
    )(my_dp.astype(jnp.int32).reshape(1), down, *shards)


def on_device(
    tokens, experts, replicas, route_weights, slot_tables, partners, slot_rows, gate_w, up_w, down_w
):
    steps, tok, model = tokens.shape
    top = experts.shape[-1]
    n_dp = lax.axis_size("dp")
    columns = lax.axis_size("x") * lax.axis_size("y")
    quad = lax.axis_size("zh") * lax.axis_size("core")
    me = lax.axis_index("zh") * lax.axis_size("core") + lax.axis_index("core")
    column = lax.axis_index("x") * lax.axis_size("y") + lax.axis_index("y")
    my_home = column * quad + me
    my_dp = lax.axis_index("dp")
    mine = steps * tok
    group = quad * tok
    boxes = columns * quad * MOST
    wide = model + LANES
    width = down_w.shape[2]

    right = [[(i, i + 1) for i in range(j, n_dp - 1)] for j in range(n_dp - 1)]
    left = [[(i + 1, i) for i in range(n_dp - 1 - j)] for j in range(n_dp - 1)]

    meta = pack_meta(
        experts.reshape(mine, top),
        replicas.reshape(mine, top),
        route_weights.reshape(mine, top),
        slot_tables[0],
    )
    packed = jnp.concatenate([tokens.reshape(mine, model), meta], axis=1)
    held = lax.all_gather(packed.reshape(steps, tok, wide), ("zh", "core"), axis=1, tiled=True)

    labels = jnp.arange(partners.shape[0], dtype=jnp.int32)
    partner_me = jnp.sum(jnp.where(labels == my_home, partners, 0))
    owners = (my_home, partner_me)
    lanes = jnp.arange(LANES, dtype=jnp.int32)[None, :]
    line = jnp.arange(boxes, dtype=jnp.int32)
    lower = (line[:, None] < line[None, :]).astype(BF)

    def exchange(local, after=None):
        place = places(local[:, model:], me, columns, quad, tok, top)[1]
        if after is not None:
            place = place & after
        send = lax.dot_general(
            place.astype(BF), local, (((0,), (0,)), ((), ())), preferred_element_type=F32
        ).astype(BF)
        return lax.all_to_all(
            send.reshape(columns, quad * MOST, wide),
            ("x", "y"),
            split_axis=0,
            concat_axis=0,
            tiled=True,
        ).reshape(boxes, wide)

    def compacted(arrived, local, step, after=None):
        valid = arrived[:, model + ONE]
        rank = jnp.dot(valid[None, :], lower, preferred_element_type=F32)
        which = (jnp.arange(n_dp, dtype=jnp.int32)[:, None] == my_dp) & (
            labels[None, :] == owners[step]
        )
        limit = jnp.sum(jnp.where(which, slot_rows[step], 0)).astype(F32)
        kept = (valid[None, :] > 0) & (rank < limit)
        if after is not None:
            kept = kept & after
        slot_row = jnp.arange(ROWS, dtype=jnp.int32).astype(F32)[:, None]
        chosen = kept & (rank == slot_row)
        pick = chosen.astype(BF)
        compact = jnp.dot(pick, arrived[:, :model], preferred_element_type=F32).astype(BF)
        position = jnp.sum(
            jnp.where(chosen, line.astype(F32)[None, :] + 1.0, 0.0), axis=1, keepdims=True
        )
        side = jnp.pad(local[:, model:], ((0, ROWS - group), (0, 0)))
        side = jnp.where(lanes == POS, position.astype(BF), side)
        return jnp.concatenate([compact, side], axis=1)

    both_w = jnp.concatenate([gate_w[0], up_w[0]], axis=1)
    last = n_dp - 1
    own = [None] * steps
    to_right, to_left = [None] * steps, [None] * steps
    done = [[[] for _ in range(n_dp)] for _ in range(steps)]
    own[0] = compacted(exchange(held[0]), held[0], 0)
    to_right[0], to_left[0] = own[0], own[0]
    arrived = exchange(held[1], own[0][0, 0] == own[0][0, 0])
    order = [(1, 0)]
    for j in range(2, n_dp):
        order += [(j, 0), (j - 1, 1)]
    order.append((last, 1))
    made = None
    for j, s in order:
        if (j, s) == (2, 0):
            own[1] = compacted(arrived, held[1], 1, made[0][0, 0] == made[0][0, 0])
            to_right[1], to_left[1] = own[1], own[1]
        to_right[s] = lax.ppermute(to_right[s], "dp", right[j - 1])
        to_left[s] = lax.ppermute(to_left[s], "dp", left[j - 1])
        blocks = [to_right[s], to_left[s]] + ([own[s]] if j == 1 else [])
        passed = 2 if j < last else 0
        sent, made = project(both_w, blocks, passed, [] if made is None else [made[0]])
        if passed:
            to_right[s], to_left[s] = sent
        done[s][j].append((made[0], 0, last))
        done[s][n_dp - j].append((made[1], 0, last))
        if j == 1:
            done[s][0].append((made[2], 0, last))

    partials = []
    for s in range(steps):
        hidden = assemble([done[s]], 0, my_dp)
        shards, places_of = [hidden], [lambda z: z]
        going_right, going_left = hidden, hidden
        for j in range(1, n_dp):
            going_right = lax.ppermute(going_right, "dp", right[j - 1])
            going_left = lax.ppermute(going_left, "dp", left[j - 1])
            shards += [going_right, going_left]
            places_of.append(lambda z, j=j: lax.rem(z - j + n_dp, n_dp))
            places_of.append(lambda z, j=j: lax.rem(z + j, n_dp))
        output = project_down(shards, places_of, down_w[0], n_dp, my_dp)
        sides = assemble([done[s]], LANES, my_dp).reshape(n_dp, ROWS, LANES)
        positions = sides[:, :, POS].astype(jnp.int32) - 1
        unpick = (line[None, :, None] == positions[:, None, :]).astype(BF)
        spread = jnp.einsum(
            "bpr,brf->bpf",
            unpick,
            output.reshape(n_dp, ROWS, width),
            preferred_element_type=F32,
        ).astype(BF)
        back = lax.all_to_all(
            spread.reshape(n_dp, columns, quad * MOST, width).transpose(1, 0, 2, 3),
            ("x", "y"),
            split_axis=0,
            concat_axis=0,
            tiled=True,
        )
        token_meta = sides[:, :group].reshape(n_dp * group, LANES)
        hits, place = places(token_meta, me, columns, quad, tok, top)
        parts = []
        for lane in (HI, MID):
            weight = jnp.zeros((n_dp * group, boxes), F32)
            for k in range(top):
                weight = jnp.where(
                    hits[k], token_meta[:, lane + k : lane + k + 1].astype(F32), weight
                )
            parts.append(jnp.where(place, weight, 0.0).astype(BF).reshape(n_dp, group, boxes))
        sums = jnp.einsum(
            "btp,bpf->btf",
            jnp.concatenate(parts, axis=1),
            back.transpose(1, 0, 2, 3).reshape(n_dp, boxes, width),
            preferred_element_type=F32,
        )
        partials.append((sums[:, :group] + sums[:, group:]).astype(BF))
    partial = jnp.stack(partials)
    partial = partial.reshape(steps, n_dp, 2, 2, tok, width).transpose(3, 2, 1, 0, 4, 5)
    swapped = lax.all_to_all(partial, "core", split_axis=0, concat_axis=0, tiled=True)
    halves = jnp.sum(swapped.astype(F32), axis=0).astype(BF)
    pieces = lax.all_to_all(
        halves.reshape(2 * n_dp, mine * width // LANES, LANES),
        ("zh", "dp"),
        split_axis=0,
        concat_axis=0,
        tiled=True,
    ).reshape(2, n_dp, mine, width)
    mixed = jnp.sum(pieces.astype(F32), axis=0).astype(BF)
    return mixed.transpose(1, 0, 2).reshape(steps, tok, model)


def solution(mesh):
    names = ("dp", "x", "y", "zh", "core")
    grid = Mesh(mesh.devices.reshape(mesh.shape["dp"], 4, 4, 2, 2), names)
    ep = ("x", "y", "zh", "core")
    rows = P(None, names, None)
    return jax.shard_map(
        on_device,
        mesh=grid,
        in_specs=(
            rows,
            rows,
            rows,
            rows,
            P(),
            P(),
            P(),
            P(ep, None, "dp"),
            P(ep, None, "dp"),
            P(ep, None, "dp"),
        ),
        out_specs=rows,
        check_vma=False,
    )
```

```python
import functools

import jax
import jax.numpy as jnp
from jax import lax
from jax.experimental import pallas as pl
from jax.experimental.pallas import tpu as pltpu
from jax.sharding import Mesh, PartitionSpec as P

BF = jnp.bfloat16
F32 = jnp.float32
LANES = 128
ROWS = 48
MOST = 2
HOME, HI, MID, ONE, POS = 0, 8, 16, 32, 33


def split_gates(gates):
    high = lax.reduce_precision(gates, 8, 7)
    mid = lax.reduce_precision(gates - high, 8, 7)
    return high.astype(BF), mid.astype(BF)


def pack_meta(experts, replicas, gates, table):
    labels = jnp.arange(table.shape[0], dtype=jnp.int32)
    hot = experts[..., None] == labels
    picked = jnp.where(replicas[..., None] == 0, table[:, 0], table[:, 1])
    home = jnp.sum(jnp.where(hot, picked, 0), axis=-1)
    high, mid = split_gates(gates)
    one = jnp.ones(home.shape, BF)
    meta = jnp.concatenate([home.astype(BF), high, mid, one, one], axis=-1)
    return jnp.pad(meta, ((0, 0), (0, LANES - meta.shape[-1])))


def places(meta, me, columns, quad, tok, top, sets=1):
    n = meta.shape[0]
    box = jnp.arange(columns * sets * quad * MOST, dtype=jnp.int32)[None, :]
    row = jnp.arange(n, dtype=jnp.int32)[:, None]
    target = (box // (sets * quad * MOST) * quad + me).astype(BF)
    same = (row // tok) % (sets * quad) == (box // MOST) % (sets * quad)
    hits = [(meta[:, HOME + k : HOME + k + 1] == target) & same for k in range(top)]
    match = hits[0]
    for hit in hits[1:]:
        match = match | hit
    other = jnp.arange(n, dtype=jnp.int32)[None, :]
    before = ((row // tok == other // tok) & (other < row)).astype(BF)
    earlier = jnp.dot(before, match.astype(BF), preferred_element_type=F32)
    return hits, match & (earlier == (box % MOST).astype(F32))


def project_kernel(count, passed, extra, weight_ref, *refs):
    blocks = refs[:count]
    outs = refs[count + extra + passed : 2 * count + extra + passed]
    rows_ref, sems = refs[-2:]
    width = weight_ref.shape[1] // 2
    model = weight_ref.shape[0]
    copies = [
        pltpu.make_async_copy(
            blocks[i], rows_ref.at[pl.ds(i * ROWS, ROWS)], sems.at[i]
        )
        for i in range(count)
    ]
    for copy in copies:
        copy.start()
    for copy in copies:
        copy.wait()
    both = jnp.dot(rows_ref[:, :model], weight_ref[...], preferred_element_type=F32)
    gate, up = both[:, :width], both[:, width:]
    hidden = (gate / (1.0 + jnp.exp(-gate)) * up).astype(BF)
    for i in range(count):
        outs[i][:, :width] = hidden[i * ROWS : (i + 1) * ROWS]
        outs[i][:, width:] = rows_ref[i * ROWS : (i + 1) * ROWS, model:]


SMALL = pl.CostEstimate(flops=1000, bytes_accessed=1000, transcendentals=0)


def project(weight, blocks, passed, extra=()):
    vmem = pl.BlockSpec(memory_space=pltpu.VMEM)
    there = pl.BlockSpec(memory_space=pl.ANY)
    count = len(blocks)
    out = pl.pallas_call(
        functools.partial(project_kernel, count, passed, len(extra)),
        out_shape=[jax.ShapeDtypeStruct(block.shape, BF) for block in blocks[:passed]]
        + [jax.ShapeDtypeStruct((ROWS, 2 * LANES), BF)] * count,
        in_specs=[vmem] + [there] * (count + len(extra)),
        out_specs=[there] * passed + [vmem] * count,
        input_output_aliases={1 + i: i for i in range(passed)},
        scratch_shapes=[
            pltpu.VMEM((count * ROWS, blocks[0].shape[1]), BF),
            pltpu.SemaphoreType.DMA((count,)),
        ],
        compiler_params=pltpu.CompilerParams(vmem_limit_bytes=24 * 2**20),
        cost_estimate=SMALL,
    )(weight, *blocks, *extra)
    return out[:passed], out[passed:]


def assemble_kernel(plan, low, n_dp, dp_ref, *refs):
    out_ref = refs[-1]
    z = dp_ref[0]
    for s, m, members in plan:
        value = None
        for index, least, most in members:
            part = refs[index][:, low : low + LANES]
            if least > 0 or most < n_dp - 1:
                here = ((z >= least) & (z <= most)).astype(F32)
                part = (part.astype(F32) * here).astype(BF)
            value = part if value is None else value + part
        spot = s * n_dp + lax.rem(z - m + n_dp, n_dp)
        out_ref[pl.ds(pl.multiple_of(spot * ROWS, ROWS), ROWS), :] = value


def assemble(done, low, my_dp):
    plan, flat, known = [], [], {}
    for s, slots in enumerate(done):
        for m, parts in enumerate(slots):
            members = []
            for block, least, most in parts:
                if id(block) not in known:
                    known[id(block)] = len(flat)
                    flat.append(block)
                members.append((known[id(block)], least, most))
            plan.append((s, m, members))
    n_dp = len(done[0])
    vmem = pl.BlockSpec(memory_space=pltpu.VMEM)
    return pl.pallas_call(
        functools.partial(assemble_kernel, plan, low, n_dp),
        out_shape=jax.ShapeDtypeStruct((len(plan) * ROWS, LANES), BF),
        in_specs=[pl.BlockSpec(memory_space=pltpu.SMEM)] + [vmem] * len(flat),
        out_specs=vmem,
        compiler_params=pltpu.CompilerParams(vmem_limit_bytes=8 * 2**20),
        cost_estimate=SMALL,
    )(my_dp.astype(jnp.int32).reshape(1), *flat)


def down_kernel(places_of, n_dp, dp_ref, down_ref, *refs):
    out_ref = refs[-1]
    z = dp_ref[0]
    total = None
    for i in range(0, len(places_of), 2):
        pair = range(i, min(i + 2, len(places_of)))
        weights = [
            down_ref[pl.ds(pl.multiple_of(places_of[p](z) * LANES, LANES), LANES), :] for p in pair
        ]
        part = jnp.dot(
            jnp.concatenate([refs[p][...] for p in pair], axis=1),
            jnp.concatenate(weights, axis=0),
            preferred_element_type=F32,
        )
        total = part if total is None else total + part
    out_ref[...] = total.astype(BF)


def project_down(shards, places_of, down, n_dp, my_dp):
    vmem = pl.BlockSpec(memory_space=pltpu.VMEM)
    return pl.pallas_call(
        functools.partial(down_kernel, places_of, n_dp),
        out_shape=jax.ShapeDtypeStruct((shards[0].shape[0], down.shape[1]), BF),
        in_specs=[pl.BlockSpec(memory_space=pltpu.SMEM), vmem] + [vmem] * len(shards),
        out_specs=vmem,
        compiler_params=pltpu.CompilerParams(vmem_limit_bytes=32 * 2**20),
        cost_estimate=SMALL,
    )(my_dp.astype(jnp.int32).reshape(1), down, *shards)


def on_device(
    tokens, experts, replicas, route_weights, slot_tables, partners, slot_rows, gate_w, up_w, down_w
):
    steps, tok, model = tokens.shape
    top = experts.shape[-1]
    n_dp = lax.axis_size("dp")
    columns = lax.axis_size("x") * lax.axis_size("y")
    quad = lax.axis_size("zh") * lax.axis_size("core")
    me = lax.axis_index("zh") * lax.axis_size("core") + lax.axis_index("core")
    column = lax.axis_index("x") * lax.axis_size("y") + lax.axis_index("y")
    my_home = column * quad + me
    my_dp = lax.axis_index("dp")
    mine = steps * tok
    group = quad * tok
    boxes = columns * quad * MOST
    wide = model + LANES
    width = down_w.shape[2]

    right = [[(i, i + 1) for i in range(j, n_dp - 1)] for j in range(n_dp - 1)]
    left = [[(i + 1, i) for i in range(n_dp - 1 - j)] for j in range(n_dp - 1)]

    meta = pack_meta(
        experts.reshape(mine, top),
        replicas.reshape(mine, top),
        route_weights.reshape(mine, top),
        slot_tables[0],
    )
    packed = jnp.concatenate([tokens.reshape(mine, model), meta], axis=1)
    held = lax.all_gather(packed.reshape(steps, tok, wide), ("zh", "core"), axis=1, tiled=True)

    labels = jnp.arange(partners.shape[0], dtype=jnp.int32)
    partner_me = jnp.sum(jnp.where(labels == my_home, partners, 0))
    owners = (my_home, partner_me)
    lanes = jnp.arange(LANES, dtype=jnp.int32)[None, :]
    line = jnp.arange(boxes, dtype=jnp.int32)
    lower = (line[:, None] < line[None, :]).astype(BF)

    def exchange(local, after=None):
        place = places(local[:, model:], me, columns, quad, tok, top)[1]
        if after is not None:
            place = place & after
        send = lax.dot_general(
            place.astype(BF), local, (((0,), (0,)), ((), ())), preferred_element_type=F32
        ).astype(BF)
        return lax.all_to_all(
            send.reshape(columns, quad * MOST, wide),
            ("x", "y"),
            split_axis=0,
            concat_axis=0,
            tiled=True,
        ).reshape(boxes, wide)

    def compacted(arrived, local, step, after=None):
        valid = arrived[:, model + ONE]
        rank = jnp.dot(valid[None, :], lower, preferred_element_type=F32)
        which = (jnp.arange(n_dp, dtype=jnp.int32)[:, None] == my_dp) & (
            labels[None, :] == owners[step]
        )
        limit = jnp.sum(jnp.where(which, slot_rows[step], 0)).astype(F32)
        kept = (valid[None, :] > 0) & (rank < limit)
        if after is not None:
            kept = kept & after
        slot_row = jnp.arange(ROWS, dtype=jnp.int32).astype(F32)[:, None]
        chosen = kept & (rank == slot_row)
        pick = chosen.astype(BF)
        compact = jnp.dot(pick, arrived[:, :model], preferred_element_type=F32).astype(BF)
        position = jnp.sum(
            jnp.where(chosen, line.astype(F32)[None, :] + 1.0, 0.0), axis=1, keepdims=True
        )
        side = jnp.pad(local[:, model:], ((0, ROWS - group), (0, 0)))
        side = jnp.where(lanes == POS, position.astype(BF), side)
        return jnp.concatenate([compact, side], axis=1)

    both_w = jnp.concatenate([gate_w[0], up_w[0]], axis=1)
    last = n_dp - 1
    own = [None] * steps
    to_right, to_left = [None] * steps, [None] * steps
    done = [[[] for _ in range(n_dp)] for _ in range(steps)]
    own[0] = compacted(exchange(held[0]), held[0], 0)
    to_right[0], to_left[0] = own[0], own[0]
    arrived = exchange(held[1], own[0][0, 0] == own[0][0, 0])
    order = [(1, 0)]
    for j in range(2, n_dp):
        order += [(j, 0), (j - 1, 1)]
    order.append((last, 1))
    made, made_at = None, {}
    for j, s in order:
        if (j, s) == (2, 0):
            own[1] = compacted(arrived, held[1], 1, made[0][0, 0] == made[0][0, 0])
            to_right[1], to_left[1] = own[1], own[1]
        to_right[s] = lax.ppermute(to_right[s], "dp", right[j - 1])
        to_left[s] = lax.ppermute(to_left[s], "dp", left[j - 1])
        blocks = [to_right[s], to_left[s]] + ([own[s]] if j == 1 else [])
        passed = 2 if j < last else 0
        sent, made = project(both_w, blocks, passed, [] if made is None else [made[0]])
        made_at[j, s] = made[0]
        if passed:
            to_right[s], to_left[s] = sent
        done[s][j].append((made[0], 0, last))
        done[s][n_dp - j].append((made[1], 0, last))
        if j == 1:
            done[s][0].append((made[2], 0, last))

    def behind(block, others):
        there = others[0][0, 0] == others[0][0, 0]
        for other in others[1:]:
            there = there & (other[0, 0] == other[0, 0])
        return jnp.where(there, block, jnp.zeros_like(block))

    hidden = [assemble([done[s]], 0, my_dp) for s in range(steps)]
    shards = [[hidden[s]] for s in range(steps)]
    places_of = [lambda z: z]
    for j in range(1, n_dp):
        places_of.append(lambda z, j=j: lax.rem(z - j + n_dp, n_dp))
        places_of.append(lambda z, j=j: lax.rem(z + j, n_dp))

    def pass_on(s, j, after=None):
        going = shards[s][-2:] if j > 1 else [hidden[s], hidden[s]]
        if after is not None:
            going = [behind(going[0], after), behind(going[1], after)]
        shards[s].append(lax.ppermute(going[0], "dp", right[j - 1]))
        shards[s].append(lax.ppermute(going[1], "dp", left[j - 1]))

    pass_on(0, 1)
    pass_on(0, 2, [made_at[last - 1, 1]])
    pass_on(0, 3)
    pass_on(0, 4, [made_at[last, 1]])
    for j in range(5, n_dp):
        pass_on(1, j - 4)
        pass_on(0, j, shards[1][-2:])
    for j in range(n_dp - 4, n_dp):
        pass_on(1, j)

    partials = []
    for s in range(steps):
        output = project_down(shards[s], places_of, down_w[0], n_dp, my_dp)
        sides = assemble([done[s]], LANES, my_dp).reshape(n_dp, ROWS, LANES)
        positions = sides[:, :, POS].astype(jnp.int32) - 1
        unpick = (line[None, :, None] == positions[:, None, :]).astype(BF)
        spread = jnp.einsum(
            "bpr,brf->bpf",
            unpick,
            output.reshape(n_dp, ROWS, width),
            preferred_element_type=F32,
        ).astype(BF)
        back = lax.all_to_all(
            spread.reshape(n_dp, columns, quad * MOST, width).transpose(1, 0, 2, 3),
            ("x", "y"),
            split_axis=0,
            concat_axis=0,
            tiled=True,
        )
        token_meta = sides[:, :group].reshape(n_dp * group, LANES)
        hits, place = places(token_meta, me, columns, quad, tok, top)
        parts = []
        for lane in (HI, MID):
            weight = jnp.zeros((n_dp * group, boxes), F32)
            for k in range(top):
                weight = jnp.where(
                    hits[k], token_meta[:, lane + k : lane + k + 1].astype(F32), weight
                )
            parts.append(jnp.where(place, weight, 0.0).astype(BF).reshape(n_dp, group, boxes))
        sums = jnp.einsum(
            "btp,bpf->btf",
            jnp.concatenate(parts, axis=1),
            back.transpose(1, 0, 2, 3).reshape(n_dp, boxes, width),
            preferred_element_type=F32,
        )
        partials.append((sums[:, :group] + sums[:, group:]).astype(BF))
    partial = jnp.stack(partials)
    partial = partial.reshape(steps, n_dp, 2, 2, tok, width).transpose(3, 2, 1, 0, 4, 5)
    swapped = lax.all_to_all(partial, "core", split_axis=0, concat_axis=0, tiled=True)
    halves = jnp.sum(swapped.astype(F32), axis=0).astype(BF)
    pieces = lax.all_to_all(
        halves.reshape(2 * n_dp, mine * width // LANES, LANES),
        ("zh", "dp"),
        split_axis=0,
        concat_axis=0,
        tiled=True,
    ).reshape(2, n_dp, mine, width)
    mixed = jnp.sum(pieces.astype(F32), axis=0).astype(BF)
    return mixed.transpose(1, 0, 2).reshape(steps, tok, model)


def solution(mesh):
    names = ("dp", "x", "y", "zh", "core")
    grid = Mesh(mesh.devices.reshape(mesh.shape["dp"], 4, 4, 2, 2), names)
    ep = ("x", "y", "zh", "core")
    rows = P(None, names, None)
    return jax.shard_map(
        on_device,
        mesh=grid,
        in_specs=(
            rows,
            rows,
            rows,
            rows,
            P(),
            P(),
            P(),
            P(ep, None, "dp"),
            P(ep, None, "dp"),
            P(ep, None, "dp"),
        ),
        out_specs=rows,
        check_vma=False,
    )
```

```python
import functools

import jax
import jax.numpy as jnp
from jax import lax
from jax.experimental import pallas as pl
from jax.experimental.pallas import tpu as pltpu
from jax.sharding import Mesh, PartitionSpec as P

BF = jnp.bfloat16
F32 = jnp.float32
LANES = 128
ROWS = 48
MOST = 2
EARLY = 5
HOME, HI, MID, ONE, POS = 0, 8, 16, 32, 33


def split_gates(gates):
    high = lax.reduce_precision(gates, 8, 7)
    mid = lax.reduce_precision(gates - high, 8, 7)
    return high.astype(BF), mid.astype(BF)


def pack_meta(experts, replicas, gates, table):
    labels = jnp.arange(table.shape[0], dtype=jnp.int32)
    hot = experts[..., None] == labels
    picked = jnp.where(replicas[..., None] == 0, table[:, 0], table[:, 1])
    home = jnp.sum(jnp.where(hot, picked, 0), axis=-1)
    high, mid = split_gates(gates)
    one = jnp.ones(home.shape, BF)
    meta = jnp.concatenate([home.astype(BF), high, mid, one, one], axis=-1)
    return jnp.pad(meta, ((0, 0), (0, LANES - meta.shape[-1])))


def places(meta, me, columns, quad, tok, top):
    n = meta.shape[0]
    box = jnp.arange(columns * quad * MOST, dtype=jnp.int32)[None, :]
    row = jnp.arange(n, dtype=jnp.int32)[:, None]
    target = (box // (quad * MOST) * quad + me).astype(BF)
    same = (row // tok) % quad == (box // MOST) % quad
    hits = [(meta[:, HOME + k : HOME + k + 1] == target) & same for k in range(top)]
    match = hits[0]
    for hit in hits[1:]:
        match = match | hit
    other = jnp.arange(n, dtype=jnp.int32)[None, :]
    before = ((row // tok == other // tok) & (other < row)).astype(BF)
    earlier = jnp.dot(before, match.astype(BF), preferred_element_type=F32)
    return hits, match & (earlier == (box % MOST).astype(F32))


def project_kernel(count, passed, extra, weight_ref, *refs):
    blocks = refs[:count]
    outs = refs[count + extra + passed : 2 * count + extra + passed]
    rows_ref, sems = refs[-2:]
    width = weight_ref.shape[1] // 2
    model = weight_ref.shape[0]
    copies = [
        pltpu.make_async_copy(
            blocks[i], rows_ref.at[pl.ds(i * ROWS, ROWS)], sems.at[i]
        )
        for i in range(count)
    ]
    for copy in copies:
        copy.start()
    for copy in copies:
        copy.wait()
    both = jnp.dot(rows_ref[:, :model], weight_ref[...], preferred_element_type=F32)
    gate, up = both[:, :width], both[:, width:]
    hidden = (gate / (1.0 + jnp.exp(-gate)) * up).astype(BF)
    for i in range(count):
        outs[i][:, :width] = hidden[i * ROWS : (i + 1) * ROWS]
        outs[i][:, width:] = rows_ref[i * ROWS : (i + 1) * ROWS, model:]


SMALL = pl.CostEstimate(flops=1000, bytes_accessed=1000, transcendentals=0)


def project(weight, blocks, passed, extra=()):
    vmem = pl.BlockSpec(memory_space=pltpu.VMEM)
    there = pl.BlockSpec(memory_space=pl.ANY)
    count = len(blocks)
    out = pl.pallas_call(
        functools.partial(project_kernel, count, passed, len(extra)),
        out_shape=[jax.ShapeDtypeStruct(block.shape, BF) for block in blocks[:passed]]
        + [jax.ShapeDtypeStruct((ROWS, 2 * LANES), BF)] * count,
        in_specs=[vmem] + [there] * (count + len(extra)),
        out_specs=[there] * passed + [vmem] * count,
        input_output_aliases={1 + i: i for i in range(passed)},
        scratch_shapes=[
            pltpu.VMEM((count * ROWS, blocks[0].shape[1]), BF),
            pltpu.SemaphoreType.DMA((count,)),
        ],
        compiler_params=pltpu.CompilerParams(vmem_limit_bytes=24 * 2**20),
        cost_estimate=SMALL,
    )(weight, *blocks, *extra)
    return out[:passed], out[passed:]


def assemble_kernel(plan, low, n_dp, dp_ref, *refs):
    out_ref = refs[-1]
    z = dp_ref[0]
    for (s, m), members in plan:
        value = refs[members[0]][:, low : low + LANES]
        for other in members[1:]:
            value = value + refs[other][:, low : low + LANES]
        spot = s * n_dp + lax.rem(z - m + n_dp, n_dp)
        out_ref[pl.ds(pl.multiple_of(spot * ROWS, ROWS), ROWS), :] = value


def assemble(done, low, my_dp):
    plan, flat = [], []
    for s, slots in enumerate(done):
        for m, parts in enumerate(slots):
            plan.append(((s, m), tuple(range(len(flat), len(flat) + len(parts)))))
            flat += parts
    n_dp = len(done[0])
    vmem = pl.BlockSpec(memory_space=pltpu.VMEM)
    return pl.pallas_call(
        functools.partial(assemble_kernel, plan, low, n_dp),
        out_shape=jax.ShapeDtypeStruct((len(plan) * ROWS, LANES), BF),
        in_specs=[pl.BlockSpec(memory_space=pltpu.SMEM)] + [vmem] * len(flat),
        out_specs=vmem,
        compiler_params=pltpu.CompilerParams(vmem_limit_bytes=8 * 2**20),
        cost_estimate=SMALL,
    )(my_dp.astype(jnp.int32).reshape(1), *flat)


def on_device(
    tokens, experts, replicas, route_weights, slot_tables, partners, slot_rows, gate_w, up_w, down_w
):
    steps, tok, model = tokens.shape
    top = experts.shape[-1]
    n_dp = lax.axis_size("dp")
    columns = lax.axis_size("x") * lax.axis_size("y")
    quad = lax.axis_size("zh") * lax.axis_size("core")
    me = lax.axis_index("zh") * lax.axis_size("core") + lax.axis_index("core")
    column = lax.axis_index("x") * lax.axis_size("y") + lax.axis_index("y")
    my_home = column * quad + me
    my_dp = lax.axis_index("dp")
    mine = steps * tok
    group = quad * tok
    boxes = columns * quad * MOST
    wide = model + LANES
    width = down_w.shape[2]

    right = [[(i, i + 1) for i in range(j, n_dp - 1)] for j in range(n_dp - 1)]
    left = [[(i + 1, i) for i in range(n_dp - 1 - j)] for j in range(n_dp - 1)]

    meta = pack_meta(
        experts.reshape(mine, top),
        replicas.reshape(mine, top),
        route_weights.reshape(mine, top),
        slot_tables[0],
    )
    packed = jnp.concatenate([tokens.reshape(mine, model), meta], axis=1)
    held = lax.all_gather(packed.reshape(steps, tok, wide), ("zh", "core"), axis=1, tiled=True)

    labels = jnp.arange(partners.shape[0], dtype=jnp.int32)
    partner_me = jnp.sum(jnp.where(labels == my_home, partners, 0))
    owners = (my_home, partner_me)
    lanes = jnp.arange(LANES, dtype=jnp.int32)[None, :]
    line = jnp.arange(boxes, dtype=jnp.int32)
    lower = (line[:, None] < line[None, :]).astype(BF)

    def exchange(local, after=None):
        place = places(local[:, model:], me, columns, quad, tok, top)[1]
        if after is not None:
            place = place & after
        send = lax.dot_general(
            place.astype(BF), local, (((0,), (0,)), ((), ())), preferred_element_type=F32
        ).astype(BF)
        return lax.all_to_all(
            send.reshape(columns, quad * MOST, wide),
            ("x", "y"),
            split_axis=0,
            concat_axis=0,
            tiled=True,
        ).reshape(boxes, wide)

    def compacted(step, arrived, after=None):
        valid = arrived[:, model + ONE]
        rank = jnp.dot(valid[None, :], lower, preferred_element_type=F32)
        which = (jnp.arange(n_dp, dtype=jnp.int32)[:, None] == my_dp) & (
            labels[None, :] == owners[step]
        )
        limit = jnp.sum(jnp.where(which, slot_rows[step], 0)).astype(F32)
        kept = (valid[None, :] > 0) & (rank < limit)
        if after is not None:
            kept = kept & after
        slot_row = jnp.arange(ROWS, dtype=jnp.int32).astype(F32)[:, None]
        chosen = kept & (rank == slot_row)
        pick = chosen.astype(BF)
        compact = jnp.dot(pick, arrived[:, :model], preferred_element_type=F32).astype(BF)
        position = jnp.sum(
            jnp.where(chosen, line.astype(F32)[None, :] + 1.0, 0.0), axis=1, keepdims=True
        )
        side = jnp.pad(held[step][:, model:], ((0, ROWS - group), (0, 0)))
        side = jnp.where(lanes == POS, position.astype(BF), side)
        return jnp.concatenate([compact, side], axis=1)

    both_w = jnp.concatenate([gate_w[0], up_w[0]], axis=1)
    batch = steps * n_dp
    last = n_dp - 1
    own = [None] * steps
    to_right, to_left = [None] * steps, [None] * steps
    done = [[[] for _ in range(n_dp)] for _ in range(steps)]
    far = [[None] * n_dp for _ in range(steps)]
    own[0] = compacted(0, exchange(held[0]))
    to_right[0], to_left[0] = own[0], own[0]
    arrived = exchange(held[1], own[0][0, 0] == own[0][0, 0])
    order = [(1, 0)]
    for j in range(2, n_dp):
        order += [(j, 0), (j - 1, 1)]
    order.append((last, 1))
    hidden, made, extra = None, None, []
    for j, s in order:
        if (j, s) == (2, 0):
            own[1] = compacted(1, arrived, made[0][0, 0] == made[0][0, 0])
            to_right[1], to_left[1] = own[1], own[1]
        to_right[s] = lax.ppermute(to_right[s], "dp", right[j - 1])
        to_left[s] = lax.ppermute(to_left[s], "dp", left[j - 1])
        blocks = [to_right[s], to_left[s]] + ([own[s]] if j == 1 else [])
        passed = 2 if j < last else 0
        sent, made = project(both_w, blocks, passed, extra)
        extra = [made[0]]
        if passed:
            to_right[s], to_left[s] = sent
        if j > EARLY:
            far[s][j] = made[0][:, :LANES] + made[1][:, :LANES]
        done[s][j].append(made[0])
        done[s][n_dp - j].append(made[1])
        if j == 1:
            done[s][0].append(made[2])
        if (j, s) == (EARLY, 0):
            near = [list(parts) for parts in done[0]]
        if (j, s) == (EARLY, 1):
            hidden = assemble([near, done[1]], 0, my_dp)
            extra = [made[0], hidden]
    gathered = lax.all_gather(hidden, "dp", axis=0, tiled=False).reshape(
        n_dp, steps, n_dp, ROWS, LANES
    )
    beyond = range(EARLY + 1, n_dp)
    rest = jnp.stack([jnp.stack([far[s][k] for k in beyond]) for s in range(steps)])
    rest = lax.all_to_all(
        jnp.broadcast_to(
            rest.reshape(1, steps * len(beyond) * ROWS, LANES),
            (n_dp, steps * len(beyond) * ROWS, LANES),
        ),
        "dp",
        split_axis=0,
        concat_axis=0,
        tiled=True,
    ).reshape(n_dp, steps, len(beyond), ROWS, LANES)
    for z in range(n_dp):
        for i, k in enumerate(beyond):
            for d in (z - k, z + k):
                if 0 <= d < n_dp:
                    gathered = lax.dynamic_update_slice(
                        gathered, rest[z : z + 1, :, i : i + 1], (z, 0, d, 0, 0)
                    )
    output = jnp.einsum(
        "zrh,zhf->rf",
        gathered.reshape(n_dp, batch * ROWS, LANES),
        down_w[0].reshape(n_dp, LANES, width),
        preferred_element_type=F32,
    ).astype(BF)

    sides = assemble(done, LANES, my_dp).reshape(batch, ROWS, LANES)

    positions = sides[:, :, POS].astype(jnp.int32) - 1
    unpick = (line[None, :, None] == positions[:, None, :]).astype(BF)
    spread = jnp.einsum(
        "bpr,brf->bpf",
        unpick,
        output.reshape(batch, ROWS, width),
        preferred_element_type=F32,
    ).astype(BF)
    back = lax.all_to_all(
        spread.reshape(batch, columns, quad * MOST, width).transpose(1, 0, 2, 3),
        ("x", "y"),
        split_axis=0,
        concat_axis=0,
        tiled=True,
    )

    token_meta = sides[:, :group].reshape(batch * group, LANES)
    hits, place = places(token_meta, me, columns, quad, tok, top)
    parts = []
    for lane in (HI, MID):
        weight = jnp.zeros((batch * group, boxes), F32)
        for k in range(top):
            weight = jnp.where(
                hits[k], token_meta[:, lane + k : lane + k + 1].astype(F32), weight
            )
        parts.append(jnp.where(place, weight, 0.0).astype(BF).reshape(batch, group, boxes))
    sums = jnp.einsum(
        "btp,bpf->btf",
        jnp.concatenate(parts, axis=1),
        back.transpose(1, 0, 2, 3).reshape(batch, boxes, width),
        preferred_element_type=F32,
    )
    partial = (sums[:, :group] + sums[:, group:]).astype(BF)
    partial = partial.reshape(steps, n_dp, 2, 2, tok, width).transpose(3, 2, 1, 0, 4, 5)
    swapped = lax.all_to_all(partial, "core", split_axis=0, concat_axis=0, tiled=True)
    halves = jnp.sum(swapped.astype(F32), axis=0).astype(BF)
    pieces = lax.all_to_all(
        halves.reshape(2 * n_dp, mine * width // LANES, LANES),
        ("zh", "dp"),
        split_axis=0,
        concat_axis=0,
        tiled=True,
    ).reshape(2, n_dp, mine, width)
    mixed = jnp.sum(pieces.astype(F32), axis=0).astype(BF)
    return mixed.transpose(1, 0, 2).reshape(steps, tok, model)


def solution(mesh):
    names = ("dp", "x", "y", "zh", "core")
    grid = Mesh(mesh.devices.reshape(mesh.shape["dp"], 4, 4, 2, 2), names)
    ep = ("x", "y", "zh", "core")
    rows = P(None, names, None)
    return jax.shard_map(
        on_device,
        mesh=grid,
        in_specs=(
            rows,
            rows,
            rows,
            rows,
            P(),
            P(),
            P(),
            P(ep, None, "dp"),
            P(ep, None, "dp"),
            P(ep, None, "dp"),
        ),
        out_specs=rows,
        check_vma=False,
    )
```
